128 devices in a mesh: frame: 32 (over z_hi, x, y), head: 4 (over z_lo, core).
Axes of the slice: x: 4, y: 4, z: 4 (z_hi: 2, z_lo: 2; z = z_hi * 2 + z_lo), core: 2. Of those that a mesh axis runs over, the one named last changes fastest.
Arguments:
- hidden_a: bfloat16 [128, 1024, 640], P('frame'), may hold values from -6 to 6
- w_qkv_a: bfloat16 [3, 640, 640], P(None, None, 'head'), as said below
- w_out_a: bfloat16 [640, 640], replicated, may hold values from -0.25 to 0.25
- hidden_b: bfloat16 [128, 256, 1280], P('frame'), may hold values from -6 to 6
- w_qkv_b: bfloat16 [3, 1280, 1280], P(None, None, 'head'), as said below
- w_out_b: bfloat16 [1280, 1280], replicated, may hold values from -0.15625 to 0.15625
Outputs:
- out_a: bfloat16 [128, 1024, 640], P('frame', None, 'head')
- out_b: bfloat16 [128, 256, 1280], P('frame', None, 'head')
The draws below stay inside these ranges and needn't reach their ends.
Inputs may be any that keep to these rules, and one draw needn't show every extreme that they name: `w_qkv_a`: query, key and value projections, entries independent. `w_qkv_b`: query, key and value projections, entries independent.
All inputs are finite; a program needn't handle non-finite values.
Results may differ from the reference program's by a relative error of at most 0.005.
The reference program's roundings to bfloat16 on the way count: a program that leaves them out, or rounds other values in their place, can miss the bound.
Values may be sent and summed in bfloat16 or wider, within the bound.
No kernel may reach another device: no remote copies, remote signals or barrier semaphores. Data moves between devices by JAX's collectives and lax.ppermute only.
A program may use at most 128 MiB of HBM per device.

```python
import math
import jax
import jax.numpy as jnp
from jax import lax

DA = 640
DB = 1280
HEADS = 8
SA = 1024
SB = 256
FRAMES = 128


def projection_draw(key, width, boost):
    matrix = jax.random.normal(key, (3, width, width), jnp.float32) * width ** (-0.5)
    factor = jnp.array([boost, boost, 1.0], jnp.float32)[:, None, None]
    return (matrix * factor).astype(jnp.bfloat16)


def draw_w_qkv_a(key, part):
    key = jax.random.fold_in(key, 11)
    return projection_draw(key, DA, 1.0)


def draw_w_qkv_b(key, part):
    key = jax.random.fold_in(key, 23)
    return projection_draw(key, DB, 1.0)


def block_scale(own_key, shape, shards, least, largest):
    gain, own = 1.0, jax.random.fold_in(own_key, 6)
    for axis_at, blocks in shards:
        heights = jnp.exp(jax.random.uniform(jax.random.fold_in(own, axis_at), (blocks,), jnp.float32, least / len(shards), largest / len(shards)))
        gain = gain * jnp.repeat(heights, shape[axis_at] // blocks).reshape([-1 if axis == axis_at else 1 for axis in range(len(shape))])
    return gain


def scatter_about(key, shape, scale, bound, cuts=(), dtype=jnp.bfloat16):
    level = block_scale(key, shape, cuts, -0.22, 0.18) if cuts else 1.0
    values = jax.random.normal(key, shape, jnp.float32) * scale * level
    return jnp.minimum(jnp.maximum(values, -bound), bound).astype(dtype)


def setup_inputs(seed: int = 0) -> dict:
    keys = jax.random.split(jax.random.key(seed), 7)
    hidden_a = scatter_about(keys[0], (FRAMES, SA, DA), 1.0, 6.0, ((0, 32),))
    w_qkv_a = draw_w_qkv_a(jax.random.fold_in(keys[6], 71), 0)
    w_out_a = scatter_about(keys[2], (DA, DA), DA ** -0.5, 0.25)
    hidden_b = scatter_about(keys[3], (FRAMES, SB, DB), 1.0, 6.0, ((0, 32),))
    w_qkv_b = draw_w_qkv_b(jax.random.fold_in(keys[6], 71), 0)
    w_out_b = scatter_about(keys[5], (DB, DB), DB ** -0.5, 0.15625)
    return dict(hidden_a=hidden_a, w_qkv_a=w_qkv_a, w_out_a=w_out_a, hidden_b=hidden_b, w_qkv_b=w_qkv_b, w_out_b=w_out_b)


def normalize(hidden):
    as_float = hidden.astype(jnp.float32)
    centre = lax.optimization_barrier(jnp.mean(as_float, axis=-1, keepdims=True))
    spread = lax.optimization_barrier(jnp.mean(jnp.square(as_float - centre), axis=-1, keepdims=True))
    return ((as_float - centre) * lax.rsqrt(spread + 1e-05)).astype(jnp.bfloat16)

def sublayer(hidden, w_qkv, w_out):
    frames, seq_len, width = hidden.shape
    size_head = width // HEADS
    flat_rows = normalize(hidden).reshape(frames * seq_len, width)
    parts = [jnp.dot(flat_rows, w_qkv[index], preferred_element_type=jnp.float32).astype(jnp.bfloat16).reshape(frames, seq_len, HEADS, size_head) for index in range(3)]
    queries, key_rows, value_rows = parts
    prev_keys = jnp.concatenate([key_rows[:1], key_rows[:-1]], axis=0)
    prev_values = jnp.concatenate([value_rows[:1], value_rows[:-1]], axis=0)
    score_scale = 1.0 / math.sqrt(size_head)

    def one_frame(inputs):
        query_f, prev_k, prev_v, own_k, own_v = inputs
        key_tile = jnp.concatenate([key_rows[0], prev_k, own_k], axis=0).astype(jnp.float32)
        value_tile = jnp.concatenate([value_rows[0], prev_v, own_v], axis=0).astype(jnp.float32)
        scores = jnp.einsum('qhd,khd->hqk', query_f.astype(jnp.float32), key_tile) * score_scale
        row_max = lax.optimization_barrier(jnp.max(scores, axis=-1, keepdims=True))
        weights = jnp.exp(scores - row_max)
        weights = (weights / lax.optimization_barrier(jnp.sum(weights, axis=-1, keepdims=True))).astype(jnp.bfloat16)
        return jnp.einsum('hqk,khd->qhd', weights.astype(jnp.float32), value_tile).astype(jnp.bfloat16)
    attended = lax.map(one_frame, (queries, prev_keys, prev_values, key_rows, value_rows))
    attended = attended.reshape(frames * seq_len, width)
    summed = jnp.dot(attended, w_out, preferred_element_type=jnp.float32)
    summed = summed + hidden.reshape(frames * seq_len, width).astype(jnp.float32)
    return summed.astype(jnp.bfloat16).reshape(frames, seq_len, width)

def reference(hidden_a, w_qkv_a, w_out_a, hidden_b, w_qkv_b, w_out_b):
    return (sublayer(hidden_a, w_qkv_a, w_out_a), sublayer(hidden_b, w_qkv_b, w_out_b))
```

```python
import functools
import math

import jax
import jax.numpy as jnp
from jax import lax
from jax.experimental import pallas as pl
from jax.experimental.pallas import tpu as pltpu
from jax.sharding import PartitionSpec as P

HEADS = 8
F32 = jnp.float32
BF16 = jnp.bfloat16
NT = (((1,), (1,)), ((), ()))
TN = (((0,), (0,)), ((), ()))
VMEM_LIMIT = 48 * 2**20


def params():
    return pltpu.CompilerParams(vmem_limit_bytes=VMEM_LIMIT)


def cost(flops, bytes_accessed, exps=0):
    return pl.CostEstimate(
        flops=int(flops), bytes_accessed=int(bytes_accessed), transcendentals=int(exps)
    )


def whole(array):
    return pl.BlockSpec(array.shape, lambda *_: (0,) * array.ndim)


def normalize(rows):
    as_float = rows.astype(F32)
    centre = jnp.mean(as_float, axis=-1, keepdims=True)
    moved = as_float - centre
    spread = jnp.mean(jnp.square(moved), axis=-1, keepdims=True)
    return (moved * lax.rsqrt(spread + 1e-05)).astype(BF16)


def project_body(x_ref, wqv_ref, wk_ref, q_ref, k_ref, v_ref):
    normed = normalize(x_ref[0])
    width = wk_ref.shape[1]
    both = lax.dot_general(wqv_ref[...], normed, NT, preferred_element_type=F32).astype(BF16)
    q_ref[0] = both[:width]
    v_ref[0] = both[width:]
    k_ref[0] = jnp.dot(normed, wk_ref[...], preferred_element_type=F32).astype(BF16)


def project(hidden, w_qv, w_k):
    frames, seq, width = hidden.shape
    local = w_k.shape[1]
    col = jax.ShapeDtypeStruct((frames, local, seq), BF16)
    row = jax.ShapeDtypeStruct((frames, seq, local), BF16)
    at = lambda f: (f, 0, 0)
    return pl.pallas_call(
        project_body,
        grid=(frames,),
        in_specs=[pl.BlockSpec((1, seq, width), at), whole(w_qv), whole(w_k)],
        out_specs=[
            pl.BlockSpec((1, local, seq), at),
            pl.BlockSpec((1, seq, local), at),
            pl.BlockSpec((1, local, seq), at),
        ],
        out_shape=[col, row, col],
        compiler_params=params(),
        cost_estimate=cost(2 * 4 * frames * seq * width * local, frames * seq * width * 4),
    )(hidden, w_qv, w_k)


def project_kv_body(x_ref, wv_ref, wk_ref, k_ref, v_ref):
    normed = normalize(x_ref[...])
    v_ref[...] = lax.dot_general(wv_ref[...], normed, NT, preferred_element_type=F32).astype(BF16)
    k_ref[...] = jnp.dot(normed, wk_ref[...], preferred_element_type=F32).astype(BF16)


def project_kv(rows, w_v, w_k):
    seq, width = rows.shape
    local = w_k.shape[1]
    return pl.pallas_call(
        project_kv_body,
        out_shape=[
            jax.ShapeDtypeStruct((seq, local), BF16),
            jax.ShapeDtypeStruct((local, seq), BF16),
        ],
        compiler_params=params(),
        cost_estimate=cost(2 * 3 * seq * width * local, seq * width * 4),
    )(rows, w_v, w_k)


def masked_queries(q, size):
    row = lax.broadcasted_iota(jnp.int32, q.shape, 0)
    zero = jnp.zeros_like(q)
    heads = q.shape[0] // size
    return [jnp.where((row >= h * size) & (row < (h + 1) * size), q, zero) for h in range(heads)]


def with_ones(v):
    return jnp.concatenate([v, jnp.ones((16, v.shape[1]), BF16)], axis=0)


def run_chunks(chunks, scale, tops, sums):
    def score(chunk):
        _, keys, queries, _ = chunk
        s = jnp.dot(keys, queries, preferred_element_type=F32)
        return s, jnp.max(s, axis=0, keepdims=True)

    ahead = score(chunks[0])
    for i, (h, _, _, values) in enumerate(chunks):
        s, top = ahead
        if i + 1 < len(chunks):
            ahead = score(chunks[i + 1])
        new = top if tops[h] is None else jnp.maximum(tops[h], top)
        weights = jnp.exp2((s - new) * scale).astype(BF16)
        part = jnp.dot(values, weights, preferred_element_type=F32)
        if tops[h] is not None:
            part = part + sums[h] * jnp.exp2((tops[h] - new) * scale)
        tops[h], sums[h] = new, part
    return tops, sums


def local_body(q_ref, ko_ref, vo_ref, kp_ref, vp_ref, st_ref, *, size, scale):
    queries = masked_queries(q_ref[0], size)
    chunks = []
    for h, q in enumerate(queries):
        rows = pl.ds(h * size, size)
        for k_ref, v_ref in ((ko_ref, vo_ref), (kp_ref, vp_ref)):
            chunks.append((h, k_ref[0], q, with_ones(v_ref[0, rows, :])))
    tops, sums = run_chunks(chunks, scale, [None] * len(queries), [None] * len(queries))
    for h in range(len(queries)):
        st_ref[h, : size + 8, :] = sums[h][: size + 8]
        st_ref[h, size + 8 :, :] = jnp.broadcast_to(tops[h], (8, tops[h].shape[1]))


def attend_local(frame, q, k, v, prev, size, tile):
    _, local, seq = q.shape
    heads = local // size
    own = lambda j: (frame, 0, 0)
    if prev is None:
        before, kp, vp = (lambda j: (frame - 1, 0, 0)), k, v
    else:
        before, (kp, vp) = (lambda j: (0, 0, 0)), prev
    ks, vs = (1, seq, local), (1, local, seq)
    return pl.pallas_call(
        functools.partial(local_body, size=size, scale=math.log2(math.e) / math.sqrt(size)),
        grid=(seq // tile,),
        in_specs=[
            pl.BlockSpec((1, local, tile), lambda j: (frame, 0, j)),
            pl.BlockSpec(ks, own),
            pl.BlockSpec(vs, own),
            pl.BlockSpec(ks, before),
            pl.BlockSpec(vs, before),
        ],
        out_specs=pl.BlockSpec((heads, size + 16, tile), lambda j: (0, 0, j)),
        out_shape=jax.ShapeDtypeStruct((heads, size + 16, seq), F32),
        compiler_params=params(),
        cost_estimate=cost(
            2 * 2 * heads * seq * 2 * seq * 256, 8 * seq * local, heads * 2 * seq * seq
        ),
    )(q, k, v, kp, vp)


def anchor_body(q_ref, k_ref, v_ref, st_ref, o_ref, *, size, scale):
    queries = masked_queries(q_ref[0], size)
    heads = len(queries)
    chunks = [
        (h, k_ref[...], queries[h], with_ones(v_ref[pl.ds(h * size, size), :]))
        for h in range(heads)
    ]
    sums = [
        jnp.concatenate([st_ref[h, : size + 8, :], st_ref[h, size : size + 8, :]], axis=0)
        for h in range(heads)
    ]
    tops = [st_ref[h, size + 8 : size + 9, :] for h in range(heads)]
    tops, sums = run_chunks(chunks, scale, tops, sums)
    for h in range(heads):
        o_ref[pl.ds(h * size, size), :] = (sums[h][:size] / sums[h][size : size + 1]).astype(BF16)


def attend_anchor(frame, q, k0, v0, state, size, tile):
    _, local, seq = q.shape
    heads = local // size
    return pl.pallas_call(
        functools.partial(anchor_body, size=size, scale=math.log2(math.e) / math.sqrt(size)),
        grid=(seq // tile,),
        in_specs=[
            pl.BlockSpec((1, local, tile), lambda j: (frame, 0, j)),
            whole(k0),
            whole(v0),
            pl.BlockSpec((heads, size + 16, tile), lambda j: (0, 0, j)),
        ],
        out_specs=pl.BlockSpec((local, tile), lambda j: (0, j)),
        out_shape=jax.ShapeDtypeStruct((local, seq), BF16),
        compiler_params=params(),
        cost_estimate=cost(
            2 * 2 * heads * seq * seq * 256, 8 * seq * local, heads * seq * seq
        ),
    )(q, k0, v0, state)


def small_body(q_ref, ko, vo, kl, vl, kr, vr, ka, va, o_ref, *, size, scale):
    first = pl.program_id(0) == 0
    kp = jnp.where(first, kr[...], kl[0])
    vp = jnp.where(first, vr[...], vl[0])
    queries = masked_queries(q_ref[0], size)
    chunks = []
    for h, q in enumerate(queries):
        rows = slice(h * size, (h + 1) * size)
        for keys, values in ((ko[0], vo[0]), (kp, vp), (ka[...], va[...])):
            chunks.append((h, keys, q, with_ones(values[rows])))
    _, sums = run_chunks(chunks, scale, [None] * len(queries), [None] * len(queries))
    for h in range(len(queries)):
        o_ref[pl.ds(h * size, size), :] = (sums[h][:size] / sums[h][size : size + 1]).astype(BF16)


def attend_small(q, k, v, prev, anchor, size):
    frames, local, seq = q.shape
    heads = local // size
    at = lambda f: (f, 0, 0)
    before = lambda f: (jnp.maximum(f - 1, 0), 0, 0)
    ks, vs = (1, seq, local), (1, local, seq)
    return pl.pallas_call(
        functools.partial(small_body, size=size, scale=math.log2(math.e) / math.sqrt(size)),
        grid=(frames,),
        in_specs=[
            pl.BlockSpec((1, local, seq), at),
            pl.BlockSpec(ks, at),
            pl.BlockSpec(vs, at),
            pl.BlockSpec(ks, before),
            pl.BlockSpec(vs, before),
            whole(prev[0]),
            whole(prev[1]),
            whole(anchor[0]),
            whole(anchor[1]),
        ],
        out_specs=pl.BlockSpec((local, seq), lambda f: (0, f)),
        out_shape=jax.ShapeDtypeStruct((local, frames * seq), BF16),
        compiler_params=params(),
        cost_estimate=cost(
            2 * 2 * frames * heads * seq * 3 * seq * 512, 16 * frames * seq * local,
            frames * heads * seq * 3 * seq,
        ),
    )(q, k, v, k, v, *prev, *anchor)


def out_body(own_ref, across_ref, beside_ref, w_ref, pick_ref, x_ref, *rest):
    o_ref = rest[-1]
    attended = jnp.concatenate([own_ref[...], across_ref[...], beside_ref[...]], axis=0)
    total = lax.dot_general(attended, w_ref[...], TN, preferred_element_type=F32)
    kept = jnp.dot(x_ref[0], pick_ref[...], preferred_element_type=F32)
    o_ref[0] = (total + kept).astype(BF16)


def out_project(first, frames, pieces, w, pick, hidden, into):
    total_frames, seq, width = hidden.shape
    cols = w.shape[1]
    operands = list(pieces) + [w, pick, hidden]
    specs = [pl.BlockSpec((p.shape[0], seq), lambda f: (0, f)) for p in pieces]
    specs += [whole(w), whole(pick), pl.BlockSpec((1, seq, width), lambda f: (first + f, 0, 0))]
    aliases = {}
    if into is not None:
        aliases = {len(operands): 0}
        operands.append(into)
        specs.append(pl.BlockSpec(memory_space=pl.ANY))
    return pl.pallas_call(
        out_body,
        grid=(frames,),
        in_specs=specs,
        out_specs=pl.BlockSpec((1, seq, cols), lambda f: (first + f, 0, 0)),
        out_shape=jax.ShapeDtypeStruct((total_frames, seq, cols), BF16),
        input_output_aliases=aliases,
        compiler_params=params(),
        cost_estimate=cost(2 * 2 * frames * seq * width * cols, 4 * frames * seq * width),
    )(*operands)


def tree(piece, order):
    index = lax.axis_index("frame")
    held = [0]
    for bit in order:
        got = lax.ppermute(piece, "frame", [(i, i ^ bit) for i in held])
        new = [i ^ bit for i in held]
        receives = functools.reduce(jnp.logical_or, [index == i for i in new])
        piece = jnp.where(receives, got, piece)
        held = held + new
    return piece


def head_swap(value, bit):
    peers = lax.axis_size("head")
    return lax.ppermute(value, "head", [(i, i ^ bit) for i in range(peers)])


def share_rows(rows):
    both = jnp.concatenate([rows, head_swap(rows, 2)], axis=0)
    return jnp.concatenate([both, head_swap(both, 1)], axis=0)


def gather_heads(own):
    across = head_swap(own, 2)
    beside = head_swap(jnp.concatenate([own, across], axis=0), 1)
    return own, across, beside


def from_previous(k_last, v_last, k_first, v_first):
    both = jnp.concatenate([k_last.T, v_last], axis=0)
    peers = lax.axis_size("frame")
    got = lax.ppermute(both, "frame", [(i, i + 1) for i in range(peers - 1)])
    local = v_last.shape[0]
    start = lax.axis_index("frame") == 0
    return (
        jnp.where(start, k_first, got[:local].T),
        jnp.where(start, v_first, got[local:]),
    )


def out_weights(w_out, rank, cols):
    mine = lax.dynamic_slice_in_dim(w_out, rank * cols, cols, 1)
    blocks = mine.reshape(-1, cols, cols)
    ordered = [
        lax.dynamic_index_in_dim(blocks, jnp.bitwise_xor(rank, j), 0, keepdims=False)
        for j in (0, 2, 1, 3)
    ]
    pick = (
        lax.broadcasted_iota(jnp.int32, mine.shape, 0)
        == lax.broadcasted_iota(jnp.int32, mine.shape, 1) + rank * cols
    ).astype(BF16)
    return jnp.concatenate(ordered, axis=0), pick


def quarter(hidden, rank):
    rows = hidden.shape[1] // lax.axis_size("head")
    return lax.dynamic_slice_in_dim(hidden[0], rank * rows, rows, 0)


def split_weights(w_qkv):
    local = w_qkv.shape[2]
    w_qv = jnp.concatenate([w_qkv[0].T, w_qkv[2].T], axis=0)
    return w_qv, w_qkv[1], w_qv[local:]


def shards(hidden_a, w_qkv_a, w_out_a, hidden_b, w_qkv_b, w_out_b):
    rank = lax.axis_index("head")
    frames, seq_a, _ = hidden_a.shape
    local_a, local_b = w_qkv_a.shape[2], w_qkv_b.shape[2]
    size_a, size_b = local_a // 2, local_b // 2

    rows_a = quarter(hidden_a, rank)
    half = rows_a.shape[0] // 2
    low = tree(rows_a[:half], (8, 4, 2, 1, 16))
    high = tree(rows_a[half:], (2, 1, 16, 8, 4))
    rows_b = tree(quarter(hidden_b, rank), (16, 8, 4, 2, 1))

    wqv_a, wk_a, wv_a = split_weights(w_qkv_a)
    wqv_b, wk_b, wv_b = split_weights(w_qkv_b)
    q_a, k_a, v_a = project(hidden_a, wqv_a, wk_a)
    q_b, k_b, v_b = project(hidden_b, wqv_b, wk_b)
    prev_a = from_previous(k_a[frames - 1], v_a[frames - 1], k_a[0], v_a[0])
    prev_b = from_previous(k_b[frames - 1], v_b[frames - 1], k_b[0], v_b[0])

    tile = 512
    states = [None] * frames
    for f in range(1, frames):
        states[f] = attend_local(f, q_a, k_a, v_a, None, size_a, tile)
    states[0] = attend_local(
        0, q_a, k_a, v_a, (prev_a[0][None], prev_a[1][None]), size_a, tile
    )

    anchor_b = project_kv(share_rows(rows_b), wv_b, wk_b)
    att_b = attend_small(q_b, k_b, v_b, prev_b, anchor_b, size_b)
    pieces_b = gather_heads(att_b)

    anchor_a = project_kv(share_rows(jnp.concatenate([low, high], axis=0)), wv_a, wk_a)
    w_a, pick_a = out_weights(w_out_a, rank, local_a)
    w_b, pick_b = out_weights(w_out_b, rank, local_b)
    out_a = None
    for f in (1, 2, 3, 0):
        att = attend_anchor(f, q_a, *anchor_a, states[f], size_a, tile)
        out_a = out_project(f, 1, gather_heads(att), w_a, pick_a, hidden_a, out_a)
    out_b = out_project(0, frames, pieces_b, w_b, pick_b, hidden_b, None)
    return out_a, out_b


def solution(mesh):
    in_specs = (
        P("frame", None, None),
        P(None, None, "head"),
        P(),
        P("frame", None, None),
        P(None, None, "head"),
        P(),
    )
    out_specs = (P("frame", None, "head"), P("frame", None, "head"))
    return jax.shard_map(shards, mesh=mesh, in_specs=in_specs, out_specs=out_specs, check_vma=False)
```

```python
import functools
import math

import jax
import jax.numpy as jnp
from jax import lax
from jax.experimental import pallas as pl
from jax.experimental.pallas import tpu as pltpu
from jax.sharding import PartitionSpec as P

HEADS = 8
F32 = jnp.float32
BF16 = jnp.bfloat16
NT = (((1,), (1,)), ((), ()))
ANY = pl.BlockSpec(memory_space=pl.ANY)
SMEM = pl.BlockSpec(memory_space=pltpu.SMEM)
SAFE_EXPONENT = 64.0
SAFE_VALUE = 2.0**30


def params(mib=24):
    return pltpu.CompilerParams(vmem_limit_bytes=mib * 2**20)


def cost(flops, bytes_accessed, exps=0):
    return pl.CostEstimate(
        flops=int(flops), bytes_accessed=int(bytes_accessed), transcendentals=int(exps)
    )


def whole(array):
    return pl.BlockSpec(array.shape, lambda *_: (0,) * array.ndim)


def normalize(rows):
    as_float = rows.astype(F32)
    centre = jnp.mean(as_float, axis=-1, keepdims=True)
    moved = as_float - centre
    spread = jnp.mean(jnp.square(moved), axis=-1, keepdims=True)
    return (moved * lax.rsqrt(spread + 1e-05)).astype(BF16)


def times(weights, normed):
    return lax.dot_general(weights, normed, NT, preferred_element_type=F32).astype(BF16)


def head_rows(local, size):
    row = lax.broadcasted_iota(jnp.int32, (8, local), 0)
    col = lax.broadcasted_iota(jnp.int32, (8, local), 1)
    return ((col >= row * size) & (col < (row + 1) * size)).astype(BF16)


def squares(array):
    as_float = array.astype(F32)
    return (as_float * as_float).astype(BF16)


def column_peaks(array, size):
    sums = jnp.dot(head_rows(array.shape[0], size), squares(array), preferred_element_type=F32)
    return jnp.broadcast_to(jnp.max(sums, axis=1, keepdims=True), (8, 128))


def row_peaks(array, size):
    sums = lax.dot_general(
        head_rows(array.shape[1], size), squares(array), NT, preferred_element_type=F32
    )
    return jnp.broadcast_to(jnp.max(sums, axis=1, keepdims=True), (8, 128))


def unless_extreme(peaks, values):
    largest = jnp.max(jnp.abs(values.astype(F32)))
    usual = (largest <= SAFE_VALUE) & (largest >= 1.0 / SAFE_VALUE)
    return jnp.where(usual, peaks, jnp.full_like(peaks, jnp.inf))


def within(q_peaks, k_peaks, scale):
    return jnp.max(q_peaks * k_peaks) * (1.05 * scale * scale) <= SAFE_EXPONENT**2


def project_body(x_ref, w_ref, *rest, size):
    q_ref, k_ref, v_ref, qn_ref, kn_ref, last_ref = rest[-6:]
    local = w_ref.shape[1]
    normed = normalize(x_ref[0])
    queries = times(w_ref[0], normed)
    q_ref[0] = queries
    qn_ref[0] = column_peaks(queries, size)
    keys = times(normed, w_ref[1])
    k_ref[0] = keys
    values = times(w_ref[2], normed)
    v_ref[0] = values
    kn_ref[0] = unless_extreme(row_peaks(keys, size), values)

    @pl.when(pl.program_id(0) == pl.num_programs(0) - 1)
    def _():
        last_ref[:local] = times(w_ref[1], normed)
        last_ref[local:] = values


def project(hidden, w, size, after):
    frames, seq, width = hidden.shape
    local = w.shape[1]
    col = jax.ShapeDtypeStruct((frames, local, seq), BF16)
    row = jax.ShapeDtypeStruct((frames, seq, local), BF16)
    last = jax.ShapeDtypeStruct((2 * local, seq), BF16)
    peak = jax.ShapeDtypeStruct((frames, 8, 128), F32)
    at = lambda f: (f, 0, 0)
    return pl.pallas_call(
        functools.partial(project_body, size=size),
        grid=(frames,),
        in_specs=[pl.BlockSpec((1, seq, width), at), whole(w)] + [ANY] * len(after),
        out_specs=[
            pl.BlockSpec((1, local, seq), at),
            pl.BlockSpec((1, seq, local), at),
            pl.BlockSpec((1, local, seq), at),
            pl.BlockSpec((1, 8, 128), at),
            pl.BlockSpec((1, 8, 128), at),
            whole(last),
        ],
        out_shape=[col, row, col, peak, peak, last],
        compiler_params=params(60),
        cost_estimate=cost(2 * 4 * frames * seq * width * local, frames * seq * width * 4),
    )(hidden, w, *after)


def project_kv_body(w_ref, *rest, size, rows):
    *x_refs, k_ref, v_ref, kn_ref = rest
    width = w_ref.shape[2]
    pieces = []
    for x_ref in x_refs:
        start, count, across = rows[0], rows[1], width // x_ref.shape[1]
        columns = [x_ref[start + i * count : start + (i + 1) * count] for i in range(across)]
        pieces.append(jnp.concatenate(columns, axis=1) if across > 1 else columns[0])
    normed = normalize(jnp.concatenate(pieces, axis=0))
    keys = times(normed, w_ref[1])
    k_ref[...] = keys
    values = times(w_ref[2], normed)
    v_ref[...] = values
    kn_ref[...] = unless_extreme(row_peaks(keys, size), values)


def project_kv(pieces, rows, w, size):
    seq = len(pieces) * rows[1]
    local, width = w.shape[1:]
    return pl.pallas_call(
        functools.partial(project_kv_body, size=size, rows=rows),
        out_shape=[
            jax.ShapeDtypeStruct((seq, local), BF16),
            jax.ShapeDtypeStruct((local, seq), BF16),
            jax.ShapeDtypeStruct((8, 128), F32),
        ],
        compiler_params=params(),
        cost_estimate=cost(2 * 3 * seq * width * local, seq * width * 4),
    )(w, *pieces)


def masked_queries(q, size):
    row = lax.broadcasted_iota(jnp.int32, q.shape, 0)
    zero = jnp.zeros_like(q)
    heads = q.shape[0] // size
    return [jnp.where((row >= h * size) & (row < (h + 1) * size), q, zero) for h in range(heads)]


def with_ones(v):
    return jnp.concatenate([v, jnp.ones((16, v.shape[1]), BF16)], axis=0)


def run_chunks(chunks, scale, tops, sums):
    def score(chunk):
        _, keys, queries, _ = chunk
        s = jnp.dot(keys, queries, preferred_element_type=F32)
        return s, jnp.max(s, axis=0, keepdims=True)

    ahead = score(chunks[0])
    for i, (h, _, _, values) in enumerate(chunks):
        s, top = ahead
        if i + 1 < len(chunks):
            ahead = score(chunks[i + 1])
        new = top if tops[h] is None else jnp.maximum(tops[h], top)
        weights = jnp.exp2((s - new) * scale).astype(BF16)
        part = jnp.dot(values, weights, preferred_element_type=F32)
        if tops[h] is not None:
            part = part + sums[h] * jnp.exp2((tops[h] - new) * scale)
        tops[h], sums[h] = new, part
    return tops, sums


def run_unshifted(chunks, scale, sums):
    for h, keys, queries, values in chunks:
        s = jnp.dot(keys, queries, preferred_element_type=F32)
        weights = jnp.exp2(s * scale).astype(BF16)
        part = jnp.dot(values, weights, preferred_element_type=F32)
        sums[h] = part if sums[h] is None else sums[h] + part
    return sums


def make_chunks(q, segments, size):
    queries = masked_queries(q, size)
    return [
        (h, keys, queries[h], with_ones(values[h * size : (h + 1) * size]))
        for h in range(len(queries))
        for keys, values in segments
    ]


def finish(o_ref, sums, size):
    for h in range(len(sums)):
        o_ref[pl.ds(h * size, size), :] = (sums[h][:size] / sums[h][size : size + 1]).astype(BF16)


def local_body(q_ref, ko_ref, vo_ref, qn_ref, kno_ref, kp_ref, vp_ref, knp_ref, *rest, **sizes):
    segments = ((ko_ref[0], vo_ref[0]), (kp_ref[0], vp_ref[0]))
    peaks = jnp.maximum(kno_ref[0], knp_ref[0])
    attend_to_state(q_ref[0], segments, qn_ref[0], peaks, rest[-1], **sizes)


def edge_body(first_ref, q_ref, ko_ref, vo_ref, qn_ref, kno_ref, edge_ref, *rest, **sizes):
    first = first_ref[0] == 1
    local = edge_ref.shape[0] // 2
    kt = edge_ref[:local]
    kp = jnp.where(first, ko_ref[0], kt.T)
    vp = jnp.where(first, vo_ref[0], edge_ref[local:])
    segments = ((ko_ref[0], vo_ref[0]), (kp, vp))
    peaks = unless_extreme(column_peaks(kt, sizes["size"]), vp)
    peaks = jnp.maximum(kno_ref[0], peaks)
    attend_to_state(q_ref[0], segments, qn_ref[0], peaks, rest[-1], **sizes)


def attend_to_state(q, segments, q_peaks, k_peaks, st_ref, size, scale):
    heads = q.shape[0] // size
    fits = within(q_peaks, k_peaks, scale)

    def keep(tops, sums):
        for h in range(heads):
            st_ref[h, : size + 8, :] = sums[h][: size + 8]
            st_ref[h, size + 8 :, :] = jnp.broadcast_to(tops[h], (8, q.shape[1]))

    @pl.when(fits)
    def _():
        sums = run_unshifted(make_chunks(q, segments, size), scale, [None] * heads)
        keep([jnp.zeros((1, q.shape[1]), F32)] * heads, sums)

    @pl.when(jnp.logical_not(fits))
    def _():
        chunks = make_chunks(q, segments, size)
        keep(*run_chunks(chunks, scale, [None] * heads, [None] * heads))


def attend_local(frame, qkv, edge, size, tile, after):
    q, k, v, qn, kn = qkv
    _, local, seq = q.shape
    heads = local // size
    own = lambda j: (frame, 0, 0)
    before = lambda j: (frame - 1, 0, 0)
    ks, vs, ns = (1, seq, local), (1, local, seq), (1, 8, 128)
    specs = [pl.BlockSpec((1, local, tile), lambda j: (frame, 0, j))]
    specs += [pl.BlockSpec(shape, own) for shape in (ks, vs, ns, ns)]
    if edge is None:
        body, operands = local_body, (q, k, v, qn, kn, k, v, kn)
        specs += [pl.BlockSpec(shape, before) for shape in (ks, vs, ns)]
    else:
        first, received = edge
        body, operands = edge_body, (first, q, k, v, qn, kn, received)
        specs = [SMEM] + specs + [whole(received)]
    return pl.pallas_call(
        functools.partial(body, size=size, scale=math.log2(math.e) / math.sqrt(size)),
        grid=(seq // tile,),
        in_specs=specs + [ANY] * len(after),
        out_specs=pl.BlockSpec((heads, size + 16, tile), lambda j: (0, 0, j)),
        out_shape=jax.ShapeDtypeStruct((heads, size + 16, seq), F32),
        compiler_params=params(),
        cost_estimate=cost(
            2 * 2 * heads * seq * 2 * seq * 256, 8 * seq * local, heads * 2 * seq * seq
        ),
    )(*operands, *after)


def anchor_body(q_ref, qn_ref, k_ref, v_ref, kn_ref, st_ref, *rest, size, scale):
    o_ref = rest[-1]
    heads = q_ref.shape[1] // size
    tops = [st_ref[h, size + 8 :, :] for h in range(heads)]
    unshifted = functools.reduce(jnp.maximum, [jnp.max(jnp.abs(t)) for t in tops]) == 0.0
    fits = jnp.logical_and(within(qn_ref[0], kn_ref[...], scale), unshifted)

    def start():
        chunks = make_chunks(q_ref[0], ((k_ref[...], v_ref[...]),), size)
        sums = [st_ref[h, : size + 8, :] for h in range(heads)]
        return chunks, [jnp.concatenate([s, s[size:]], axis=0) for s in sums]

    @pl.when(fits)
    def _():
        chunks, sums = start()
        finish(o_ref, run_unshifted(chunks, scale, sums), size)

    @pl.when(jnp.logical_not(fits))
    def _():
        chunks, sums = start()
        finish(o_ref, run_chunks(chunks, scale, [t[:1] for t in tops], sums)[1], size)


def attend_anchor(frame, qkv, anchor, state, size, tile):
    q, _, _, qn, _ = qkv
    _, local, seq = q.shape
    heads = local // size
    return pl.pallas_call(
        functools.partial(anchor_body, size=size, scale=math.log2(math.e) / math.sqrt(size)),
        grid=(seq // tile,),
        in_specs=[
            pl.BlockSpec((1, local, tile), lambda j: (frame, 0, j)),
            pl.BlockSpec((1, 8, 128), lambda j: (frame, 0, 0)),
            *[whole(part) for part in anchor],
            pl.BlockSpec((heads, size + 16, tile), lambda j: (0, 0, j)),
        ],
        out_specs=pl.BlockSpec((local, tile), lambda j: (0, j)),
        out_shape=jax.ShapeDtypeStruct((local, seq), BF16),
        compiler_params=params(),
        cost_estimate=cost(
            2 * 2 * heads * seq * seq * 256, 8 * seq * local, heads * seq * seq
        ),
    )(q, qn, *anchor, state)


def small_body(first_ref, q_ref, ko, vo, kl, vl, edge, ka, va, *rest, size, scale):
    o_ref = rest[-1]
    start = pl.program_id(0) == 0
    outer = jnp.logical_and(start, first_ref[0] == 0)
    local = edge.shape[0] // 2
    kp = jnp.where(outer, edge[:local].T, kl[0])
    vp = jnp.where(outer, edge[local:], vl[0])
    heads = q_ref.shape[1] // size
    segments = ((ko[0], vo[0]), (kp, vp), (ka[...], va[...]))
    chunks = make_chunks(q_ref[0], segments, size)
    finish(o_ref, run_chunks(chunks, scale, [None] * heads, [None] * heads)[1], size)


def attend_small(qkv, edge, anchor, size, after):
    q, k, v, _, _ = qkv
    frames, local, seq = q.shape
    heads = local // size
    at = lambda f: (f, 0, 0)
    before = lambda f: (jnp.maximum(f - 1, 0), 0, 0)
    ks, vs = (1, seq, local), (1, local, seq)
    return pl.pallas_call(
        functools.partial(small_body, size=size, scale=math.log2(math.e) / math.sqrt(size)),
        grid=(frames,),
        in_specs=[
            SMEM,
            pl.BlockSpec((1, local, seq), at),
            pl.BlockSpec(ks, at),
            pl.BlockSpec(vs, at),
            pl.BlockSpec(ks, before),
            pl.BlockSpec(vs, before),
            whole(edge[1]),
            whole(anchor[0]),
            whole(anchor[1]),
        ]
        + [ANY] * len(after),
        out_specs=pl.BlockSpec((local, seq), lambda f: (0, f)),
        out_shape=jax.ShapeDtypeStruct((local, frames * seq), BF16),
        compiler_params=params(),
        cost_estimate=cost(
            2 * 2 * frames * heads * seq * 3 * seq * 512,
            16 * frames * seq * local,
            frames * heads * seq * 3 * seq,
        ),
    )(edge[0], q, k, v, k, v, edge[1], *anchor[:2], *after)


def out_body(rank_ref, *rest):
    pieces, (w_ref, x_ref), o_ref = rest[:4], rest[4:6], rest[-3]
    w_own, attended = rest[-2:]
    rank = rank_ref[0]
    cols, width = w_own.shape
    pick = (
        lax.broadcasted_iota(jnp.int32, (cols, width), 1)
        == lax.broadcasted_iota(jnp.int32, (cols, width), 0) + rank * cols
    ).astype(BF16)

    @pl.when(pl.program_id(0) == 0)
    def _():
        w_own[...] = times(pick, w_ref[...])

    for bit, piece in zip((0, 2, 1, 3), pieces):
        start = pl.multiple_of(jnp.bitwise_xor(rank, bit) * cols, cols)
        attended[pl.ds(start, cols), :] = piece[...]
    total = jnp.dot(w_own[...], attended[...], preferred_element_type=F32)
    kept = lax.dot_general(pick, x_ref[0], NT, preferred_element_type=F32)
    o_ref[0] = (total + kept).astype(BF16)


def out_project(first, frames, rank, pieces, w, hidden, into, after):
    total_frames, seq, width = hidden.shape
    cols = pieces[0].shape[0]
    operands = [rank, *pieces, w, hidden]
    specs = [SMEM] + [pl.BlockSpec((cols, seq), lambda f: (0, f)) for _ in pieces]
    specs += [whole(w), pl.BlockSpec((1, seq, width), lambda f: (first + f, 0, 0))]
    aliases = {}
    if into is not None:
        aliases = {len(operands): 0}
        operands.append(into)
        specs.append(ANY)
    return pl.pallas_call(
        out_body,
        grid=(frames,),
        in_specs=specs + [ANY] * len(after),
        out_specs=pl.BlockSpec((1, cols, seq), lambda f: (first + f, 0, 0)),
        out_shape=jax.ShapeDtypeStruct((total_frames, cols, seq), BF16),
        scratch_shapes=[pltpu.VMEM((cols, width), BF16), pltpu.VMEM((width, seq), BF16)],
        input_output_aliases=aliases,
        compiler_params=params(),
        cost_estimate=cost(2 * 2 * frames * seq * width * cols, 4 * frames * seq * width),
    )(*operands, *after)


def tree_step(piece, held, bits, done):
    heads = lax.axis_size("head")
    index, core = lax.axis_index("frame"), lax.axis_index("head") % 2
    pairs, masks, after = [], [], []
    for mine, bit in zip(held, bits):
        after.append(mine + [i ^ bit for i in mine])
        masks.append(sum(1 << (i ^ bit) for i in mine))
    for head in range(heads):
        bit = bits[head % 2]
        to = head ^ 2 if bit == 16 else head
        pairs += [(i * heads + head, (i ^ bit) * heads + to) for i in held[head % 2]]
    got = lax.ppermute(piece, ("frame", "head"), pairs)
    got, done = lax.optimization_barrier((got, done))
    mask = jnp.where(core == 0, jnp.uint32(masks[0]), jnp.uint32(masks[1]))
    receives = (mask >> index.astype(jnp.uint32)) & 1 == 1
    return jnp.where(receives, got, piece), after, done


def head_swap(value, bit):
    peers = lax.axis_size("head")
    return lax.ppermute(value, "head", [(i, i ^ bit) for i in range(peers)])


def gather_heads(own):
    across = head_swap(own, 2)
    return own, across, head_swap(own, 1), head_swap(across, 1)


def to_next(value):
    peers = lax.axis_size("frame")
    return lax.ppermute(value, "frame", [(i, i + 1) for i in range(peers - 1)])


def quarter(hidden, rank):
    rows = hidden.shape[1] // lax.axis_size("head")
    return lax.dynamic_slice(hidden, (0, rank * rows, 0), (1, rows, hidden.shape[2]))[0]


def shards(hidden_a, w_qkv_a, w_out_a, hidden_b, w_qkv_b, w_out_b):
    rank = lax.axis_index("head")
    rank_cell = rank.astype(jnp.int32).reshape(1)
    first_cell = (lax.axis_index("frame") == 0).astype(jnp.int32).reshape(1)
    w_a, w_b = jnp.swapaxes(w_qkv_a, 1, 2), jnp.swapaxes(w_qkv_b, 1, 2)
    frames = hidden_a.shape[0]
    size_a, size_b = w_a.shape[1] // 2, w_b.shape[1] // 2
    tile = 512

    rows_a, rows_b = quarter(hidden_a, rank), quarter(hidden_b, rank)
    width = rows_a.shape[1]
    columns = [rows_b[:, i : i + width] for i in range(0, rows_b.shape[1], width)]
    rows = jnp.concatenate([rows_a, *columns], axis=0)
    held = [[0], [0]]
    orders = list(zip((16, 8, 4, 2, 1), (2, 1, 16, 8, 4)))

    *qkv_a, last_a = project(hidden_a, w_a, size_a, ())
    rows, held, last_a = tree_step(rows, held, orders[0], last_a)
    *qkv_b, last_b = project(hidden_b, w_b, size_b, (rows,))
    rows, held, last_b = tree_step(rows, held, orders[1], last_b)
    edge_a, edge_b = (first_cell, to_next(last_a)), (first_cell, to_next(last_b))
    states = [None] * frames
    for f, bits in zip(range(1, frames), orders[2:]):
        states[f] = attend_local(f, qkv_a, None, size_a, tile, (rows,))
        rows, held, states[f] = tree_step(rows, held, bits, states[f])
    states[0] = attend_local(0, qkv_a, edge_a, size_a, tile, (rows,))

    shared = gather_heads(rows)
    anchor_b = project_kv(shared, (rows_a.shape[0], rows_b.shape[0]), w_b, size_b)
    att_b = attend_small(qkv_b, edge_b, anchor_b, size_b, ())
    pieces_b = gather_heads(att_b)

    anchor_a = project_kv(shared, (0, rows_a.shape[0]), w_a, size_a)
    out_a = None
    pieces = {}
    order = [*range(1, frames), 0]
    for f in order:
        att = attend_anchor(f, qkv_a, anchor_a, states[f], size_a, tile)
        pieces[f] = gather_heads(att)
    out_b = out_project(0, frames, rank_cell, pieces_b, w_out_b, hidden_b, None, ())
    for f in order:
        out_a = out_project(f, 1, rank_cell, pieces[f], w_out_a, hidden_a, out_a, ())
    return jnp.swapaxes(out_a, 1, 2), jnp.swapaxes(out_b, 1, 2)


def solution(mesh):
    in_specs = (
        P("frame", None, None),
        P(None, None, "head"),
        P(),
        P("frame", None, None),
        P(None, None, "head"),
        P(),
    )
    out_specs = (P("frame", None, "head"), P("frame", None, "head"))
    return jax.shard_map(shards, mesh=mesh, in_specs=in_specs, out_specs=out_specs, check_vma=False)
```

```python
import functools
import math

import jax
import jax.numpy as jnp
from jax import lax
from jax.experimental import pallas as pl
from jax.experimental.pallas import tpu as pltpu
from jax.sharding import PartitionSpec as P

HEADS = 8
F32 = jnp.float32
BF16 = jnp.bfloat16
NT = (((1,), (1,)), ((), ()))
ANY = pl.BlockSpec(memory_space=pl.ANY)
SMEM = pl.BlockSpec(memory_space=pltpu.SMEM)
SAFE_EXPONENT = 64.0
SAFE_VALUE = 2.0**30


def params(mib=24):
    return pltpu.CompilerParams(vmem_limit_bytes=mib * 2**20)


def cost(flops, bytes_accessed, exps=0):
    return pl.CostEstimate(
        flops=int(flops), bytes_accessed=int(bytes_accessed), transcendentals=int(exps)
    )


def whole(array):
    return pl.BlockSpec(array.shape, lambda *_: (0,) * len(array.shape))


def stored(shape):
    return pltpu.HBM(shape.shape, shape.dtype)


def far(array):
    return pltpu.with_memory_space_constraint(array, pltpu.HBM)


def normalize(rows):
    as_float = rows.astype(F32)
    centre = jnp.mean(as_float, axis=-1, keepdims=True)
    moved = as_float - centre
    spread = jnp.mean(jnp.square(moved), axis=-1, keepdims=True)
    return (moved * lax.rsqrt(spread + 1e-05)).astype(BF16)


def times(weights, normed):
    return lax.dot_general(weights, normed, NT, preferred_element_type=F32).astype(BF16)


def head_rows(local, size):
    row = lax.broadcasted_iota(jnp.int32, (8, local), 0)
    col = lax.broadcasted_iota(jnp.int32, (8, local), 1)
    return ((col >= row * size) & (col < (row + 1) * size)).astype(BF16)


def squares(array):
    as_float = array.astype(F32)
    return (as_float * as_float).astype(BF16)


def column_peaks(array, size):
    sums = jnp.dot(head_rows(array.shape[0], size), squares(array), preferred_element_type=F32)
    return jnp.broadcast_to(jnp.max(sums, axis=1, keepdims=True), (8, 128))


def row_peaks(array, size):
    sums = lax.dot_general(
        head_rows(array.shape[1], size), squares(array), NT, preferred_element_type=F32
    )
    return jnp.broadcast_to(jnp.max(sums, axis=1, keepdims=True), (8, 128))


def unless_extreme(peaks, values):
    largest = jnp.max(jnp.abs(values.astype(F32)))
    usual = (largest <= SAFE_VALUE) & (largest >= 1.0 / SAFE_VALUE)
    return jnp.where(usual, peaks, jnp.full_like(peaks, jnp.inf))


def within(q_peaks, k_peaks, scale):
    return jnp.max(q_peaks * k_peaks) * (1.05 * scale * scale) <= SAFE_EXPONENT**2


def project_body(x_ref, w_ref, *rest, size):
    q_ref, k_ref, v_ref, qn_ref, kn_ref, last_ref = rest[-6:]
    local = w_ref.shape[1]
    normed = normalize(x_ref[0])
    queries = times(w_ref[0], normed)
    q_ref[0] = queries
    qn_ref[0] = column_peaks(queries, size)
    keys = times(normed, w_ref[1])
    k_ref[0] = keys
    values = times(w_ref[2], normed)
    v_ref[0] = values
    kn_ref[0] = unless_extreme(row_peaks(keys, size), values)

    @pl.when(pl.program_id(0) == pl.num_programs(0) - 1)
    def _():
        last_ref[:local] = times(w_ref[1], normed)
        last_ref[local:] = values


def project(hidden, w, size, after):
    frames, seq, width = hidden.shape
    local = w.shape[1]
    col = jax.ShapeDtypeStruct((frames, local, seq), BF16)
    row = jax.ShapeDtypeStruct((frames, seq, local), BF16)
    last = jax.ShapeDtypeStruct((2 * local, seq), BF16)
    peak = jax.ShapeDtypeStruct((frames, 8, 128), F32)
    at = lambda f: (f, 0, 0)
    return pl.pallas_call(
        functools.partial(project_body, size=size),
        grid=(frames,),
        in_specs=[pl.BlockSpec((1, seq, width), at), whole(w)] + [SMEM] * len(after),
        out_specs=[
            pl.BlockSpec((1, local, seq), at),
            pl.BlockSpec((1, seq, local), at),
            pl.BlockSpec((1, local, seq), at),
            pl.BlockSpec((1, 8, 128), at),
            pl.BlockSpec((1, 8, 128), at),
            whole(last),
        ],
        out_shape=[stored(shape) for shape in (col, row, col, peak, peak, last)],
        compiler_params=params(),
        cost_estimate=cost(2 * 4 * frames * seq * width * local, frames * seq * width * 4),
    )(far(hidden), far(w), *after)


def project_kv_body(w_ref, *rest, size, rows):
    *x_refs, k_ref, v_ref, kn_ref = rest
    width = w_ref.shape[2]
    pieces = []
    for x_ref in x_refs:
        start, count, across = rows[0], rows[1], width // x_ref.shape[1]
        columns = [x_ref[start + i * count : start + (i + 1) * count] for i in range(across)]
        pieces.append(jnp.concatenate(columns, axis=1) if across > 1 else columns[0])
    normed = normalize(jnp.concatenate(pieces, axis=0))
    keys = times(normed, w_ref[1])
    k_ref[...] = keys
    values = times(w_ref[2], normed)
    v_ref[...] = values
    kn_ref[...] = unless_extreme(row_peaks(keys, size), values)


def project_kv(pieces, rows, w, size):
    seq = len(pieces) * rows[1]
    local, width = w.shape[1:]
    return pl.pallas_call(
        functools.partial(project_kv_body, size=size, rows=rows),
        out_shape=[
            jax.ShapeDtypeStruct((seq, local), BF16),
            jax.ShapeDtypeStruct((local, seq), BF16),
            jax.ShapeDtypeStruct((8, 128), F32),
        ],
        compiler_params=params(),
        cost_estimate=cost(2 * 3 * seq * width * local, seq * width * 4),
    )(w, *pieces)


def masked_queries(q, size):
    row = lax.broadcasted_iota(jnp.int32, q.shape, 0)
    zero = jnp.zeros_like(q)
    heads = q.shape[0] // size
    return [jnp.where((row >= h * size) & (row < (h + 1) * size), q, zero) for h in range(heads)]


def with_ones(v):
    return jnp.concatenate([v, jnp.ones((16, v.shape[1]), BF16)], axis=0)


def run_chunks(chunks, scale, tops, sums):
    def score(chunk):
        _, keys, queries, _ = chunk
        s = jnp.dot(keys, queries, preferred_element_type=F32)
        return s, jnp.max(s, axis=0, keepdims=True)

    ahead = score(chunks[0])
    for i, (h, _, _, values) in enumerate(chunks):
        s, top = ahead
        if i + 1 < len(chunks):
            ahead = score(chunks[i + 1])
        new = top if tops[h] is None else jnp.maximum(tops[h], top)
        weights = jnp.exp2((s - new) * scale).astype(BF16)
        part = jnp.dot(values, weights, preferred_element_type=F32)
        if tops[h] is not None:
            part = part + sums[h] * jnp.exp2((tops[h] - new) * scale)
        tops[h], sums[h] = new, part
    return tops, sums


def run_unshifted(chunks, scale, sums):
    for h, keys, queries, values in chunks:
        s = jnp.dot(keys, queries, preferred_element_type=F32)
        weights = jnp.exp2(s * scale).astype(BF16)
        part = jnp.dot(values, weights, preferred_element_type=F32)
        sums[h] = part if sums[h] is None else sums[h] + part
    return sums


def make_chunks(q, segments, size):
    queries = masked_queries(q, size)
    return [
        (h, keys, queries[h], with_ones(values[h * size : (h + 1) * size]))
        for h in range(len(queries))
        for keys, values in segments
    ]


def finish(o_ref, sums, size):
    for h in range(len(sums)):
        o_ref[pl.ds(h * size, size), :] = (sums[h][:size] / sums[h][size : size + 1]).astype(BF16)


def project_frame(x_ref, w_ref, q_ref, k_ref, v_ref, qn_ref, kn_ref, size):
    normed = normalize(x_ref[0])
    queries = times(w_ref[0], normed)
    q_ref[...] = queries
    qn_ref[...] = column_peaks(queries, size)
    keys = times(normed, w_ref[1])
    k_ref[...] = keys
    values = times(w_ref[2], normed)
    v_ref[...] = values
    kn_ref[...] = unless_extreme(row_peaks(keys, size), values)
    return normed


def first_body(x_ref, w_ref, *rest, size):
    last_ref = rest[-1]
    normed = project_frame(x_ref, w_ref, *rest[-6:-1], size)
    local = w_ref.shape[1]
    last_ref[:local] = times(w_ref[1], normed)
    last_ref[local:] = rest[-4][...]


def step_body(x_ref, w_ref, qt_ref, q1, k1, v1, qn1, kn1, *rest, size, scale):
    st_ref = rest[-1]
    k_ref, v_ref, kn_ref = rest[-5], rest[-4], rest[-2]

    @pl.when(pl.program_id(0) == 0)
    def _():
        project_frame(x_ref, w_ref, *rest[-6:-1], size)

    segments = ((k1[...], v1[...]), (k_ref[...], v_ref[...]))
    peaks = jnp.maximum(kn1[...], kn_ref[...])
    attend_to_state(qt_ref[...], segments, qn1[...], peaks, st_ref, size, scale)


def frame_shapes(seq, local):
    return [
        jax.ShapeDtypeStruct((local, seq), BF16),
        jax.ShapeDtypeStruct((seq, local), BF16),
        jax.ShapeDtypeStruct((local, seq), BF16),
        jax.ShapeDtypeStruct((8, 128), F32),
        jax.ShapeDtypeStruct((8, 128), F32),
    ]


def project_last(hidden, w, size, after):
    frames, seq, width = hidden.shape
    local = w.shape[1]
    shapes = frame_shapes(seq, local) + [jax.ShapeDtypeStruct((2 * local, seq), BF16)]
    *qkv, last = pl.pallas_call(
        functools.partial(first_body, size=size),
        grid=(1,),
        in_specs=[pl.BlockSpec((1, seq, width), lambda j: (frames - 1, 0, 0)), whole(w)]
        + [SMEM] * len(after),
        out_specs=[whole(shape) for shape in shapes],
        out_shape=[stored(shape) for shape in shapes],
        compiler_params=params(),
        cost_estimate=cost(2 * 4 * seq * width * local, seq * width * 4),
    )(far(hidden), far(w), *after)
    return qkv, last


def frame_step(frame, hidden, w, later, size, tile, after):
    _, seq, width = hidden.shape
    local = w.shape[1]
    heads = local // size
    shapes = frame_shapes(seq, local)
    state = jax.ShapeDtypeStruct((heads, size + 16, seq), F32)
    *qkv, state = pl.pallas_call(
        functools.partial(step_body, size=size, scale=math.log2(math.e) / math.sqrt(size)),
        grid=(seq // tile,),
        in_specs=[
            pl.BlockSpec((1, seq, width), lambda j: (frame, 0, 0)),
            whole(w),
            pl.BlockSpec((local, tile), lambda j: (0, j)),
            *[whole(part) for part in later],
        ]
        + [SMEM] * len(after),
        out_specs=[whole(shape) for shape in shapes]
        + [pl.BlockSpec((heads, size + 16, tile), lambda j: (0, 0, j))],
        out_shape=[stored(shape) for shape in shapes + [state]],
        compiler_params=params(),
        cost_estimate=cost(
            2 * 2 * heads * seq * 2 * seq * 256, 8 * seq * width, heads * 2 * seq * seq
        ),
    )(far(hidden), far(w), *map(far, (later[0], *later)), *after)
    return qkv, state


def edge_body(first_ref, q_ref, ko_ref, vo_ref, qn_ref, kno_ref, edge_ref, *rest, **sizes):
    first = first_ref[0] == 1
    local = edge_ref.shape[0] // 2
    kt = edge_ref[:local]
    kp = jnp.where(first, ko_ref[...], kt.T)
    vp = jnp.where(first, vo_ref[...], edge_ref[local:])
    segments = ((ko_ref[...], vo_ref[...]), (kp, vp))
    peaks = unless_extreme(column_peaks(kt, sizes["size"]), vp)
    peaks = jnp.maximum(kno_ref[...], peaks)
    attend_to_state(q_ref[...], segments, qn_ref[...], peaks, rest[-1], **sizes)


def attend_to_state(q, segments, q_peaks, k_peaks, st_ref, size, scale):
    heads = q.shape[0] // size
    fits = within(q_peaks, k_peaks, scale)

    def keep(tops, sums):
        for h in range(heads):
            st_ref[h, : size + 8, :] = sums[h][: size + 8]
            st_ref[h, size + 8 :, :] = jnp.broadcast_to(tops[h], (8, q.shape[1]))

    @pl.when(fits)
    def _():
        sums = run_unshifted(make_chunks(q, segments, size), scale, [None] * heads)
        keep([jnp.zeros((1, q.shape[1]), F32)] * heads, sums)

    @pl.when(jnp.logical_not(fits))
    def _():
        chunks = make_chunks(q, segments, size)
        keep(*run_chunks(chunks, scale, [None] * heads, [None] * heads))


def attend_edge(qkv, edge, size, tile, after):
    q, k, v, qn, kn = qkv
    local, seq = q.shape
    heads = local // size
    first, received = edge
    return pl.pallas_call(
        functools.partial(edge_body, size=size, scale=math.log2(math.e) / math.sqrt(size)),
        grid=(seq // tile,),
        in_specs=[SMEM, pl.BlockSpec((local, tile), lambda j: (0, j))]
        + [whole(part) for part in (k, v, qn, kn, received)]
        + [SMEM] * len(after),
        out_specs=pl.BlockSpec((heads, size + 16, tile), lambda j: (0, 0, j)),
        out_shape=pltpu.HBM((heads, size + 16, seq), F32),
        compiler_params=params(),
        cost_estimate=cost(
            2 * 2 * heads * seq * 2 * seq * 256, 8 * seq * local, heads * 2 * seq * seq
        ),
    )(first, *map(far, (q, k, v, qn, kn, received)), *after)


def anchor_body(q_ref, qn_ref, k_ref, v_ref, kn_ref, st_ref, *rest, size, scale):
    o_ref = rest[-1]
    heads = q_ref.shape[0] // size
    tops = [st_ref[h, size + 8 :, :] for h in range(heads)]
    unshifted = functools.reduce(jnp.maximum, [jnp.max(jnp.abs(t)) for t in tops]) == 0.0
    fits = jnp.logical_and(within(qn_ref[...], kn_ref[...], scale), unshifted)

    def start():
        chunks = make_chunks(q_ref[...], ((k_ref[...], v_ref[...]),), size)
        sums = [st_ref[h, : size + 8, :] for h in range(heads)]
        return chunks, [jnp.concatenate([s, s[size:]], axis=0) for s in sums]

    @pl.when(fits)
    def _():
        chunks, sums = start()
        finish(o_ref, run_unshifted(chunks, scale, sums), size)

    @pl.when(jnp.logical_not(fits))
    def _():
        chunks, sums = start()
        finish(o_ref, run_chunks(chunks, scale, [t[:1] for t in tops], sums)[1], size)


def attend_anchor(qkv, anchor, state, size, tile):
    q, _, _, qn, _ = qkv
    local, seq = q.shape
    heads = local // size
    return pl.pallas_call(
        functools.partial(anchor_body, size=size, scale=math.log2(math.e) / math.sqrt(size)),
        grid=(seq // tile,),
        in_specs=[
            pl.BlockSpec((local, tile), lambda j: (0, j)),
            whole(qn),
            *[whole(part) for part in anchor],
            pl.BlockSpec((heads, size + 16, tile), lambda j: (0, 0, j)),
        ],
        out_specs=pl.BlockSpec((local, tile), lambda j: (0, j)),
        out_shape=jax.ShapeDtypeStruct((local, seq), BF16),
        compiler_params=params(),
        cost_estimate=cost(
            2 * 2 * heads * seq * seq * 256, 8 * seq * local, heads * seq * seq
        ),
    )(q, qn, *anchor, state)


def small_body(first_ref, q_ref, ko, vo, kl, vl, edge, ka, va, *rest, size, scale):
    o_ref = rest[-1]
    start = pl.program_id(0) == 0
    outer = jnp.logical_and(start, first_ref[0] == 0)
    local = edge.shape[0] // 2
    kp = jnp.where(outer, edge[:local].T, kl[0])
    vp = jnp.where(outer, edge[local:], vl[0])
    heads = q_ref.shape[1] // size
    segments = ((ko[0], vo[0]), (kp, vp), (ka[...], va[...]))
    chunks = make_chunks(q_ref[0], segments, size)
    finish(o_ref, run_chunks(chunks, scale, [None] * heads, [None] * heads)[1], size)


def attend_small(qkv, edge, anchor, size, after):
    q, k, v, _, _ = qkv
    frames, local, seq = q.shape
    heads = local // size
    at = lambda f: (f, 0, 0)
    before = lambda f: (jnp.maximum(f - 1, 0), 0, 0)
    ks, vs = (1, seq, local), (1, local, seq)
    return pl.pallas_call(
        functools.partial(small_body, size=size, scale=math.log2(math.e) / math.sqrt(size)),
        grid=(frames,),
        in_specs=[
            SMEM,
            pl.BlockSpec((1, local, seq), at),
            pl.BlockSpec(ks, at),
            pl.BlockSpec(vs, at),
            pl.BlockSpec(ks, before),
            pl.BlockSpec(vs, before),
            whole(edge[1]),
            whole(anchor[0]),
            whole(anchor[1]),
        ]
        + [SMEM] * len(after),
        out_specs=pl.BlockSpec((local, seq), lambda f: (0, f)),
        out_shape=jax.ShapeDtypeStruct((local, frames * seq), BF16),
        compiler_params=params(),
        cost_estimate=cost(
            2 * 2 * frames * heads * seq * 3 * seq * 512,
            16 * frames * seq * local,
            frames * heads * seq * 3 * seq,
        ),
    )(edge[0], q, k, v, k, v, edge[1], *anchor[:2], *after)


def out_body(rank_ref, *rest):
    pieces, (w_ref, x_ref), o_ref = rest[:4], rest[4:6], rest[-3]
    w_own, attended = rest[-2:]
    rank = rank_ref[0]
    cols, width = w_own.shape
    pick = (
        lax.broadcasted_iota(jnp.int32, (cols, width), 1)
        == lax.broadcasted_iota(jnp.int32, (cols, width), 0) + rank * cols
    ).astype(BF16)

    @pl.when(pl.program_id(0) == 0)
    def _():
        w_own[...] = times(pick, w_ref[...])

    for bit, piece in zip((0, 2, 1, 3), pieces):
        start = pl.multiple_of(jnp.bitwise_xor(rank, bit) * cols, cols)
        attended[pl.ds(start, cols), :] = piece[...]
    total = jnp.dot(w_own[...], attended[...], preferred_element_type=F32)
    kept = lax.dot_general(pick, x_ref[0], NT, preferred_element_type=F32)
    o_ref[0] = (total + kept).astype(BF16)


def out_project(first, frames, rank, pieces, w, hidden, into, after):
    total_frames, seq, width = hidden.shape
    cols = pieces[0].shape[0]
    operands = [rank, *pieces, w, hidden]
    specs = [SMEM] + [pl.BlockSpec((cols, seq), lambda f: (0, f)) for _ in pieces]
    specs += [whole(w), pl.BlockSpec((1, seq, width), lambda f: (first + f, 0, 0))]
    aliases = {}
    if into is not None:
        aliases = {len(operands): 0}
        operands.append(into)
        specs.append(ANY)
    return pl.pallas_call(
        out_body,
        grid=(frames,),
        in_specs=specs + [SMEM] * len(after),
        out_specs=pl.BlockSpec((1, cols, seq), lambda f: (first + f, 0, 0)),
        out_shape=jax.ShapeDtypeStruct((total_frames, cols, seq), BF16),
        scratch_shapes=[pltpu.VMEM((cols, width), BF16), pltpu.VMEM((width, seq), BF16)],
        input_output_aliases=aliases,
        compiler_params=params(),
        cost_estimate=cost(2 * 2 * frames * seq * width * cols, 4 * frames * seq * width),
    )(*operands, *after)


def choose_body(receives_ref, got_ref, piece_ref, o_ref):
    o_ref[...] = jnp.where(receives_ref[0] == 1, got_ref[...], piece_ref[...])


def choose(receives, got, piece):
    return pl.pallas_call(
        choose_body,
        grid=(1,),
        in_specs=[SMEM, whole(got), whole(piece)],
        out_specs=whole(piece),
        out_shape=jax.ShapeDtypeStruct(piece.shape, piece.dtype),
        compiler_params=params(),
        cost_estimate=cost(0, 3 * 2 * piece.size),
    )(receives, got, piece)


def tree_step(piece, held, bits, done):
    heads = lax.axis_size("head")
    index, core = lax.axis_index("frame"), lax.axis_index("head") % 2
    pairs, masks, after = [], [], []
    for mine, bit in zip(held, bits):
        after.append(mine + [i ^ bit for i in mine])
        masks.append(sum(1 << (i ^ bit) for i in mine))
    for head in range(heads):
        bit = bits[head % 2]
        to = head ^ 2 if bit == 16 else head
        pairs += [(i * heads + head, (i ^ bit) * heads + to) for i in held[head % 2]]
    got = lax.ppermute(piece, ("frame", "head"), pairs)
    got, done = lax.optimization_barrier((got, done))
    mask = jnp.where(core == 0, jnp.uint32(masks[0]), jnp.uint32(masks[1]))
    receives = ((mask >> index.astype(jnp.uint32)) & 1).astype(jnp.int32).reshape(1)
    return choose(receives, got, piece), after, done


def head_swap(value, bit):
    peers = lax.axis_size("head")
    return lax.ppermute(value, "head", [(i, i ^ bit) for i in range(peers)])


def gather_heads(own):
    across = head_swap(own, 2)
    return own, across, head_swap(own, 1), head_swap(across, 1)


def to_next(value):
    peers = lax.axis_size("frame")
    return lax.ppermute(value, "frame", [(i, i + 1) for i in range(peers - 1)])


def quarter(hidden, rank):
    rows = hidden.shape[1] // lax.axis_size("head")
    return lax.dynamic_slice(hidden, (0, rank * rows, 0), (1, rows, hidden.shape[2]))[0]


def shards(hidden_a, w_qkv_a, w_out_a, hidden_b, w_qkv_b, w_out_b):
    rank = lax.axis_index("head")
    rank_cell = rank.astype(jnp.int32).reshape(1)
    first_cell = (lax.axis_index("frame") == 0).astype(jnp.int32).reshape(1)
    w_a, w_b = jnp.swapaxes(w_qkv_a, 1, 2), jnp.swapaxes(w_qkv_b, 1, 2)
    frames = hidden_a.shape[0]
    size_a, size_b = w_a.shape[1] // 2, w_b.shape[1] // 2
    tile = 512

    rows_a, rows_b = quarter(hidden_a, rank), quarter(hidden_b, rank)
    width = rows_a.shape[1]
    columns = [rows_b[:, i : i + width] for i in range(0, rows_b.shape[1], width)]
    rows = jnp.concatenate([rows_a, *columns], axis=0)
    held = [[0], [0]]
    orders = list(zip((16, 8, 4, 2, 1), (2, 1, 16, 8, 4)))

    qkv_a, states = [None] * frames, [None] * frames
    cell = first_cell
    qkv_a[-1], last_a = project_last(hidden_a, w_a, size_a, (cell,))
    rows, held, last_a = tree_step(rows, held, orders[0], last_a)
    edge_a = (first_cell, to_next(last_a))
    for f, bits in zip(reversed(range(frames - 1)), orders[1:]):
        rows, cell = lax.optimization_barrier((rows, cell))
        qkv_a[f], states[f + 1] = frame_step(f, hidden_a, w_a, qkv_a[f + 1], size_a, tile, (cell,))
        rows, held, states[f + 1] = tree_step(rows, held, bits, states[f + 1])
    rows, cell = lax.optimization_barrier((rows, cell))
    *qkv_b, last_b = project(hidden_b, w_b, size_b, (cell,))
    rows, held, last_b = tree_step(rows, held, orders[4], last_b)
    edge_b = (first_cell, to_next(last_b))
    rows, cell = lax.optimization_barrier((rows, cell))
    states[0] = attend_edge(qkv_a[0], edge_a, size_a, tile, (cell,))

    across = head_swap(rows, 2)
    across, states[0] = lax.optimization_barrier((across, states[0]))
    shared = (rows, across, head_swap(rows, 1), head_swap(across, 1))
    order = [*range(1, frames), 0]
    attended, crossing = {}, {}
    anchor_a = project_kv(shared, (0, rows_a.shape[0]), w_a, size_a)
    for f in order:
        attended[f] = attend_anchor(qkv_a[f], anchor_a, states[f], size_a, tile)
        crossing[f] = head_swap(attended[f], 2)
        if f == order[0]:
            anchor_b = project_kv(shared, (rows_a.shape[0], rows_b.shape[0]), w_b, size_b)
            att_b = attend_small(qkv_b, edge_b, anchor_b, size_b, ())
            crossing_b = head_swap(att_b, 2)

    out_a = out_b = None
    crossing[order[0]], attended = lax.optimization_barrier((crossing[order[0]], attended))
    for f in order:
        if out_a is not None:
            crossing[f], out_a = lax.optimization_barrier((crossing[f], out_a))
        pieces = (
            attended[f], crossing[f], head_swap(attended[f], 1), head_swap(crossing[f], 1)
        )
        out_a = out_project(f, 1, rank_cell, pieces, w_out_a, hidden_a, out_a, ())
        if f == order[0]:
            crossing_b, out_a = lax.optimization_barrier((crossing_b, out_a))
            pieces_b = (att_b, crossing_b, head_swap(att_b, 1), head_swap(crossing_b, 1))
            out_b = out_project(0, frames, rank_cell, pieces_b, w_out_b, hidden_b, None, ())
            out_a, out_b = lax.optimization_barrier((out_a, out_b))
    return jnp.swapaxes(out_a, 1, 2), jnp.swapaxes(out_b, 1, 2)


def solution(mesh):
    in_specs = (
        P("frame", None, None),
        P(None, None, "head"),
        P(),
        P("frame", None, None),
        P(None, None, "head"),
        P(),
    )
    out_specs = (P("frame", None, "head"), P("frame", None, "head"))
    return jax.shard_map(shards, mesh=mesh, in_specs=in_specs, out_specs=out_specs, check_vma=False)
```

```python
import functools
import math

import jax
import jax.numpy as jnp
from jax import lax
from jax.experimental import pallas as pl
from jax.experimental.pallas import tpu as pltpu
from jax.sharding import PartitionSpec as P

HEADS = 8
F32 = jnp.float32
BF16 = jnp.bfloat16
NT = (((1,), (1,)), ((), ()))
ANY = pl.BlockSpec(memory_space=pl.ANY)
SMEM = pl.BlockSpec(memory_space=pltpu.SMEM)
SAFE_EXPONENT = 64.0
SAFE_VALUE = 2.0**30


def params(mib=24):
    return pltpu.CompilerParams(vmem_limit_bytes=mib * 2**20)


def cost(flops, bytes_accessed, exps=0):
    return pl.CostEstimate(
        flops=int(flops), bytes_accessed=int(bytes_accessed), transcendentals=int(exps)
    )


def whole(array):
    return pl.BlockSpec(array.shape, lambda *_: (0,) * len(array.shape))


def stored(shape):
    return pltpu.HBM(shape.shape, shape.dtype)


def far(array):
    return pltpu.with_memory_space_constraint(array, pltpu.HBM)


def normalize(rows):
    as_float = rows.astype(F32)
    centre = jnp.mean(as_float, axis=-1, keepdims=True)
    moved = as_float - centre
    spread = jnp.mean(jnp.square(moved), axis=-1, keepdims=True)
    return (moved * lax.rsqrt(spread + 1e-05)).astype(BF16)


def times(weights, normed):
    return lax.dot_general(weights, normed, NT, preferred_element_type=F32).astype(BF16)


def head_rows(local, size):
    row = lax.broadcasted_iota(jnp.int32, (8, local), 0)
    col = lax.broadcasted_iota(jnp.int32, (8, local), 1)
    return ((col >= row * size) & (col < (row + 1) * size)).astype(BF16)


def squares(array):
    as_float = array.astype(F32)
    return (as_float * as_float).astype(BF16)


def column_peaks(array, size):
    sums = jnp.dot(head_rows(array.shape[0], size), squares(array), preferred_element_type=F32)
    return jnp.broadcast_to(jnp.max(sums, axis=1, keepdims=True), (8, 128))


def row_peaks(array, size):
    sums = lax.dot_general(
        head_rows(array.shape[1], size), squares(array), NT, preferred_element_type=F32
    )
    return jnp.broadcast_to(jnp.max(sums, axis=1, keepdims=True), (8, 128))


def unless_extreme(peaks, values):
    largest = jnp.max(jnp.abs(values.astype(F32)))
    usual = (largest <= SAFE_VALUE) & (largest >= 1.0 / SAFE_VALUE)
    return jnp.where(usual, peaks, jnp.full_like(peaks, jnp.inf))


def within(q_peaks, k_peaks, scale):
    return jnp.max(q_peaks * k_peaks) * (1.05 * scale * scale) <= SAFE_EXPONENT**2


def project_body(x_ref, w_ref, *rest, size):
    q_ref, k_ref, v_ref, qn_ref, kn_ref, last_ref = rest[-6:]
    local = w_ref.shape[1]
    normed = normalize(x_ref[0])
    queries = times(w_ref[0], normed)
    q_ref[0] = queries
    qn_ref[0] = column_peaks(queries, size)
    keys = times(normed, w_ref[1])
    k_ref[0] = keys
    values = times(w_ref[2], normed)
    v_ref[0] = values
    kn_ref[0] = unless_extreme(row_peaks(keys, size), values)

    @pl.when(pl.program_id(0) == pl.num_programs(0) - 1)
    def _():
        last_ref[:local] = times(w_ref[1], normed)
        last_ref[local:] = values


def project(hidden, w, size, after):
    frames, seq, width = hidden.shape
    local = w.shape[1]
    col = jax.ShapeDtypeStruct((frames, local, seq), BF16)
    row = jax.ShapeDtypeStruct((frames, seq, local), BF16)
    last = jax.ShapeDtypeStruct((2 * local, seq), BF16)
    peak = jax.ShapeDtypeStruct((frames, 8, 128), F32)
    at = lambda f: (f, 0, 0)
    return pl.pallas_call(
        functools.partial(project_body, size=size),
        grid=(frames,),
        in_specs=[pl.BlockSpec((1, seq, width), at), whole(w)] + [SMEM] * len(after),
        out_specs=[
            pl.BlockSpec((1, local, seq), at),
            pl.BlockSpec((1, seq, local), at),
            pl.BlockSpec((1, local, seq), at),
            pl.BlockSpec((1, 8, 128), at),
            pl.BlockSpec((1, 8, 128), at),
            whole(last),
        ],
        out_shape=[stored(shape) for shape in (col, row, col, peak, peak, last)],
        compiler_params=params(),
        cost_estimate=cost(2 * 4 * frames * seq * width * local, frames * seq * width * 4),
    )(far(hidden), far(w), *after)


def project_kv_body(w_ref, *rest, size, rows):
    *x_refs, k_ref, v_ref, kn_ref = rest
    width = w_ref.shape[2]
    pieces = []
    for x_ref in x_refs:
        start, count, across = rows[0], rows[1], width // x_ref.shape[1]
        columns = [x_ref[start + i * count : start + (i + 1) * count] for i in range(across)]
        pieces.append(jnp.concatenate(columns, axis=1) if across > 1 else columns[0])
    normed = normalize(jnp.concatenate(pieces, axis=0))
    keys = times(normed, w_ref[1])
    k_ref[...] = keys
    values = times(w_ref[2], normed)
    v_ref[...] = values
    kn_ref[...] = unless_extreme(row_peaks(keys, size), values)


def project_kv(pieces, rows, w, size):
    seq = len(pieces) * rows[1]
    local, width = w.shape[1:]
    return pl.pallas_call(
        functools.partial(project_kv_body, size=size, rows=rows),
        out_shape=[
            jax.ShapeDtypeStruct((seq, local), BF16),
            jax.ShapeDtypeStruct((local, seq), BF16),
            jax.ShapeDtypeStruct((8, 128), F32),
        ],
        compiler_params=params(),
        cost_estimate=cost(2 * 3 * seq * width * local, seq * width * 4),
    )(w, *pieces)


def masked_queries(q, size):
    row = lax.broadcasted_iota(jnp.int32, q.shape, 0)
    zero = jnp.zeros_like(q)
    heads = q.shape[0] // size
    return [jnp.where((row >= h * size) & (row < (h + 1) * size), q, zero) for h in range(heads)]


def with_ones(v):
    return jnp.concatenate([v, jnp.ones((16, v.shape[1]), BF16)], axis=0)


def run_chunks(chunks, scale, tops, sums):
    def score(chunk):
        _, keys, queries, _ = chunk
        s = jnp.dot(keys, queries, preferred_element_type=F32)
        return s, jnp.max(s, axis=0, keepdims=True)

    ahead = score(chunks[0])
    for i, (h, _, _, values) in enumerate(chunks):
        s, top = ahead
        if i + 1 < len(chunks):
            ahead = score(chunks[i + 1])
        new = top if tops[h] is None else jnp.maximum(tops[h], top)
        weights = jnp.exp2((s - new) * scale).astype(BF16)
        part = jnp.dot(values, weights, preferred_element_type=F32)
        if tops[h] is not None:
            part = part + sums[h] * jnp.exp2((tops[h] - new) * scale)
        tops[h], sums[h] = new, part
    return tops, sums


def run_unshifted(chunks, scale, sums):
    for h, keys, queries, values in chunks:
        s = jnp.dot(keys, queries, preferred_element_type=F32)
        weights = jnp.exp2(s * scale).astype(BF16)
        part = jnp.dot(values, weights, preferred_element_type=F32)
        sums[h] = part if sums[h] is None else sums[h] + part
    return sums


def make_chunks(q, segments, size):
    queries = masked_queries(q, size)
    return [
        (h, keys, queries[h], with_ones(values[h * size : (h + 1) * size]))
        for h in range(len(queries))
        for keys, values in segments
    ]


def finish(o_ref, sums, size):
    for h in range(len(sums)):
        o_ref[pl.ds(h * size, size), :] = (sums[h][:size] / sums[h][size : size + 1]).astype(BF16)


def project_frame(x_ref, w_ref, q_ref, k_ref, v_ref, qn_ref, kn_ref, size):
    normed = normalize(x_ref[0])
    if q_ref is not None:
        queries = times(w_ref[0], normed)
        q_ref[...] = queries
        qn_ref[...] = column_peaks(queries, size)
    keys = times(normed, w_ref[1])
    k_ref[...] = keys
    values = times(w_ref[2], normed)
    v_ref[...] = values
    kn_ref[...] = unless_extreme(row_peaks(keys, size), values)
    return normed


def first_body(x_ref, w_ref, *rest, size):
    project_frame(x_ref, w_ref, *rest[-5:], size)


def step_body(x_ref, w_ref, qt_ref, k1, v1, qn1, kn1, *rest, size, scale, edge):
    if edge:
        k_ref, v_ref, kn_ref, st_ref = rest[-4:]
        results = (None, k_ref, v_ref, None, kn_ref)
    else:
        _, k_ref, v_ref, _, kn_ref, st_ref = rest[-6:]
        results = rest[-6:-1]

    @pl.when(pl.program_id(0) == 0)
    def _():
        project_frame(x_ref, w_ref, *results, size)

    segments = ((k1[...], v1[...]), (k_ref[...], v_ref[...]))
    peaks = jnp.maximum(kn1[...], kn_ref[...])
    attend_to_state(qt_ref[...], segments, qn1[...], peaks, st_ref, size, scale)


def frame_shapes(seq, local):
    return [
        jax.ShapeDtypeStruct((local, seq), BF16),
        jax.ShapeDtypeStruct((seq, local), BF16),
        jax.ShapeDtypeStruct((local, seq), BF16),
        jax.ShapeDtypeStruct((8, 128), F32),
        jax.ShapeDtypeStruct((8, 128), F32),
    ]


def project_first(rows, w, size, after):
    _, seq, width = rows.shape
    local = w.shape[1]
    shapes = frame_shapes(seq, local)
    return pl.pallas_call(
        functools.partial(first_body, size=size),
        grid=(1,),
        in_specs=[pl.BlockSpec((1, seq, width), lambda j: (0, 0, 0)), whole(w)]
        + [SMEM] * len(after),
        out_specs=[whole(shape) for shape in shapes],
        out_shape=[stored(shape) for shape in shapes],
        compiler_params=params(),
        cost_estimate=cost(2 * 3 * seq * width * local, seq * width * 4),
    )(far(rows), far(w), *after)


def frame_step(hidden, w, later, size, tile, after, edge=False):
    _, seq, width = hidden.shape
    local = w.shape[1]
    heads = local // size
    shapes = frame_shapes(seq, local)
    if edge:
        shapes = [shapes[1], shapes[2], shapes[4]]
    state = jax.ShapeDtypeStruct((heads, size + 16, seq), F32)
    *qkv, state = pl.pallas_call(
        functools.partial(
            step_body, size=size, scale=math.log2(math.e) / math.sqrt(size), edge=edge
        ),
        grid=(seq // tile,),
        in_specs=[
            pl.BlockSpec((1, seq, width), lambda j: (0, 0, 0)),
            whole(w),
            pl.BlockSpec((local, tile), lambda j: (0, j)),
            *[whole(part) for part in later[1:]],
        ]
        + [SMEM] * len(after),
        out_specs=[whole(shape) for shape in shapes]
        + [pl.BlockSpec((heads, size + 16, tile), lambda j: (0, 0, j))],
        out_shape=[stored(shape) for shape in shapes + [state]],
        compiler_params=params(),
        cost_estimate=cost(
            2 * 2 * heads * seq * 2 * seq * 256, 8 * seq * width, heads * 2 * seq * seq
        ),
    )(far(hidden), far(w), *map(far, later), *after)
    return qkv, state


def attend_to_state(q, segments, q_peaks, k_peaks, st_ref, size, scale):
    heads = q.shape[0] // size
    fits = within(q_peaks, k_peaks, scale)

    def keep(tops, sums):
        for h in range(heads):
            st_ref[h, : size + 8, :] = sums[h][: size + 8]
            st_ref[h, size + 8 :, :] = jnp.broadcast_to(tops[h], (8, q.shape[1]))

    @pl.when(fits)
    def _():
        sums = run_unshifted(make_chunks(q, segments, size), scale, [None] * heads)
        keep([jnp.zeros((1, q.shape[1]), F32)] * heads, sums)

    @pl.when(jnp.logical_not(fits))
    def _():
        chunks = make_chunks(q, segments, size)
        keep(*run_chunks(chunks, scale, [None] * heads, [None] * heads))


def anchor_body(q_ref, qn_ref, k_ref, v_ref, kn_ref, st_ref, *rest, size, scale):
    o_ref = rest[-1]
    heads = q_ref.shape[0] // size
    tops = [st_ref[h, size + 8 :, :] for h in range(heads)]
    unshifted = functools.reduce(jnp.maximum, [jnp.max(jnp.abs(t)) for t in tops]) == 0.0
    fits = jnp.logical_and(within(qn_ref[...], kn_ref[...], scale), unshifted)

    def start():
        chunks = make_chunks(q_ref[...], ((k_ref[...], v_ref[...]),), size)
        sums = [st_ref[h, : size + 8, :] for h in range(heads)]
        return chunks, [jnp.concatenate([s, s[size:]], axis=0) for s in sums]

    @pl.when(fits)
    def _():
        chunks, sums = start()
        finish(o_ref, run_unshifted(chunks, scale, sums), size)

    @pl.when(jnp.logical_not(fits))
    def _():
        chunks, sums = start()
        finish(o_ref, run_chunks(chunks, scale, [t[:1] for t in tops], sums)[1], size)


def attend_anchor(qkv, anchor, state, size, tile):
    q, _, _, qn, _ = qkv
    local, seq = q.shape
    heads = local // size
    return pl.pallas_call(
        functools.partial(anchor_body, size=size, scale=math.log2(math.e) / math.sqrt(size)),
        grid=(seq // tile,),
        in_specs=[
            pl.BlockSpec((local, tile), lambda j: (0, j)),
            whole(qn),
            *[whole(part) for part in anchor],
            pl.BlockSpec((heads, size + 16, tile), lambda j: (0, 0, j)),
        ],
        out_specs=pl.BlockSpec((local, tile), lambda j: (0, j)),
        out_shape=jax.ShapeDtypeStruct((local, seq), BF16),
        compiler_params=params(),
        cost_estimate=cost(
            2 * 2 * heads * seq * seq * 256, 8 * seq * local, heads * seq * seq
        ),
    )(q, qn, *anchor, state)


def small_body(first_ref, q_ref, ko, vo, kl, vl, edge, ka, va, *rest, size, scale):
    o_ref = rest[-1]
    start = pl.program_id(0) == 0
    outer = jnp.logical_and(start, first_ref[0] == 0)
    local = edge.shape[0] // 2
    kp = jnp.where(outer, edge[:local].T, kl[0])
    vp = jnp.where(outer, edge[local:], vl[0])
    heads = q_ref.shape[1] // size
    segments = ((ko[0], vo[0]), (kp, vp), (ka[...], va[...]))
    chunks = make_chunks(q_ref[0], segments, size)
    finish(o_ref, run_chunks(chunks, scale, [None] * heads, [None] * heads)[1], size)


def attend_small(qkv, edge, anchor, size, after):
    q, k, v, _, _ = qkv
    frames, local, seq = q.shape
    heads = local // size
    at = lambda f: (f, 0, 0)
    before = lambda f: (jnp.maximum(f - 1, 0), 0, 0)
    ks, vs = (1, seq, local), (1, local, seq)
    return pl.pallas_call(
        functools.partial(small_body, size=size, scale=math.log2(math.e) / math.sqrt(size)),
        grid=(frames,),
        in_specs=[
            SMEM,
            pl.BlockSpec((1, local, seq), at),
            pl.BlockSpec(ks, at),
            pl.BlockSpec(vs, at),
            pl.BlockSpec(ks, before),
            pl.BlockSpec(vs, before),
            whole(edge[1]),
            whole(anchor[0]),
            whole(anchor[1]),
        ]
        + [SMEM] * len(after),
        out_specs=pl.BlockSpec((local, seq), lambda f: (0, f)),
        out_shape=jax.ShapeDtypeStruct((local, frames * seq), BF16),
        compiler_params=params(),
        cost_estimate=cost(
            2 * 2 * frames * heads * seq * 3 * seq * 512,
            16 * frames * seq * local,
            frames * heads * seq * 3 * seq,
        ),
    )(edge[0], q, k, v, k, v, edge[1], *anchor[:2], *after)


def out_body(rank_ref, *rest):
    pieces, (w_ref, x_ref), o_ref = rest[:4], rest[4:6], rest[-3]
    w_own, attended = rest[-2:]
    rank = rank_ref[0]
    cols, width = w_own.shape
    pick = (
        lax.broadcasted_iota(jnp.int32, (cols, width), 1)
        == lax.broadcasted_iota(jnp.int32, (cols, width), 0) + rank * cols
    ).astype(BF16)

    @pl.when(pl.program_id(0) == 0)
    def _():
        w_own[...] = times(pick, w_ref[...])

    for bit, piece in zip((0, 2, 1, 3), pieces):
        start = pl.multiple_of(jnp.bitwise_xor(rank, bit) * cols, cols)
        attended[pl.ds(start, cols), :] = piece[...]
    total = jnp.dot(w_own[...], attended[...], preferred_element_type=F32)
    kept = lax.dot_general(pick, x_ref[0], NT, preferred_element_type=F32)
    o_ref[0] = (total + kept).astype(BF16)


def out_project(first, frames, rank, pieces, w, hidden, into, after):
    total_frames, seq, width = hidden.shape
    cols = pieces[0].shape[0]
    operands = [rank, *pieces, w, hidden]
    specs = [SMEM] + [pl.BlockSpec((cols, seq), lambda f: (0, f)) for _ in pieces]
    specs += [whole(w), pl.BlockSpec((1, seq, width), lambda f: (first + f, 0, 0))]
    aliases = {}
    if into is not None:
        aliases = {len(operands): 0}
        operands.append(into)
        specs.append(ANY)
    return pl.pallas_call(
        out_body,
        grid=(frames,),
        in_specs=specs + [SMEM] * len(after),
        out_specs=pl.BlockSpec((1, cols, seq), lambda f: (first + f, 0, 0)),
        out_shape=jax.ShapeDtypeStruct((total_frames, cols, seq), BF16),
        scratch_shapes=[pltpu.VMEM((cols, width), BF16), pltpu.VMEM((width, seq), BF16)],
        input_output_aliases=aliases,
        compiler_params=params(),
        cost_estimate=cost(2 * 2 * frames * seq * width * cols, 4 * frames * seq * width),
    )(*operands, *after)


def choose_body(receives_ref, got_ref, piece_ref, o_ref):
    o_ref[...] = jnp.where(receives_ref[0] == 1, got_ref[...], piece_ref[...])


def choose(receives, got, piece):
    return pl.pallas_call(
        choose_body,
        grid=(1,),
        in_specs=[SMEM, whole(got), whole(piece)],
        out_specs=whole(piece),
        out_shape=jax.ShapeDtypeStruct(piece.shape, piece.dtype),
        compiler_params=params(),
        cost_estimate=cost(0, 3 * 2 * piece.size),
    )(receives, got, piece)


def tree_step(piece, held, bits, done):
    heads = lax.axis_size("head")
    index, core = lax.axis_index("frame"), lax.axis_index("head") % 2
    pairs, masks, after = [], [], []
    for mine, bit in zip(held, bits):
        after.append(mine + [i ^ bit for i in mine])
        masks.append(sum(1 << (i ^ bit) for i in mine))
    for head in range(heads):
        bit = bits[head % 2]
        to = head ^ 2 if bit == 16 else head
        pairs += [(i * heads + head, (i ^ bit) * heads + to) for i in held[head % 2]]
    got = lax.ppermute(piece, ("frame", "head"), pairs)
    got, done = lax.optimization_barrier((got, done))
    mask = jnp.where(core == 0, jnp.uint32(masks[0]), jnp.uint32(masks[1]))
    receives = ((mask >> index.astype(jnp.uint32)) & 1).astype(jnp.int32).reshape(1)
    return choose(receives, got, piece), after, done


def head_swap(value, bit):
    peers = lax.axis_size("head")
    return lax.ppermute(value, "head", [(i, i ^ bit) for i in range(peers)])


def to_next(value):
    peers = lax.axis_size("frame")
    return lax.ppermute(value, "frame", [(i, i + 1) for i in range(peers - 1)])


def to_next_low(value):
    heads, peers = lax.axis_size("head"), lax.axis_size("frame")
    pairs = [
        (i * heads + h, (i + 1) * heads + h) for i in range(peers - 1) for h in range(heads // 2)
    ]
    return lax.ppermute(value, ("frame", "head"), pairs)


def take(hidden, frame):
    return lax.dynamic_slice(hidden, (frame, 0, 0), (1, *hidden.shape[1:]))


def edge_rows(hidden, rank):
    frames, seq, width = hidden.shape
    start = (frames - 1, (rank % 2) * (seq // 2), 0)
    return lax.dynamic_slice(hidden, start, (1, seq // 2, width))[0]


def quarter(hidden, rank):
    rows = hidden.shape[1] // lax.axis_size("head")
    return lax.dynamic_slice(hidden, (0, rank * rows, 0), (1, rows, hidden.shape[2]))[0]


def shards(hidden_a, w_qkv_a, w_out_a, hidden_b, w_qkv_b, w_out_b):
    rank = lax.axis_index("head")
    rank_cell = rank.astype(jnp.int32).reshape(1)
    first_cell = (lax.axis_index("frame") == 0).astype(jnp.int32).reshape(1)
    w_a, w_b = jnp.swapaxes(w_qkv_a, 1, 2), jnp.swapaxes(w_qkv_b, 1, 2)
    frames = hidden_a.shape[0]
    size_a, size_b = w_a.shape[1] // 2, w_b.shape[1] // 2
    tile = 512

    rows_a, rows_b = quarter(hidden_a, rank), quarter(hidden_b, rank)
    width = rows_a.shape[1]
    columns = [rows_b[:, i : i + width] for i in range(0, rows_b.shape[1], width)]
    rows = jnp.concatenate([rows_a, *columns], axis=0)
    held = [[0], [0]]
    orders = list(zip((8, 4, 16, 2, 1), (2, 1, 8, 4, 16)))

    cell = first_cell
    side = rank // 2
    w_sets = (w_a, head_swap(w_a, 2))
    low, high = (take(hidden_a, 2 * side + k) for k in range(2))

    def tied(value, cell):
        return lax.optimization_barrier((value, cell))

    tops, states = [None, None], {}
    tops[0] = list(project_first(high, w_sets[0], size_a, (cell,)))
    rows, held, tops[0][3] = tree_step(rows, held, orders[0], tops[0][3])
    rest, tops[0][3] = tied(edge_rows(hidden_a, rank), tops[0][3])
    edge_a = to_next_low(rest)

    rows, cell = tied(rows, cell)
    lows = [None, None]
    lows[0], states[1, 0] = frame_step(low, w_sets[0], tops[0], size_a, tile, (cell,))
    rows, held, states[1, 0] = tree_step(rows, held, orders[1], states[1, 0])

    rows, cell = tied(rows, cell)
    *qkv_b, last_b = project(hidden_b, w_b, size_b, (cell,))
    rows, held, last_b = tree_step(rows, held, orders[2], last_b)
    edge_b = to_next(last_b)

    rows, cell = tied(rows, cell)
    edge_a, cell = tied(edge_a, cell)
    tops[1] = project_first(high, w_sets[1], size_a, (cell,))
    lows[1], states[1, 1] = frame_step(low, w_sets[1], tops[1], size_a, tile, (cell,))
    rows, held, states[1, 1] = tree_step(rows, held, orders[3], states[1, 1])

    edge_a, states[1, 1] = tied(edge_a, states[1, 1])
    received = jnp.concatenate([edge_a, head_swap(edge_a, 1)], axis=0)
    outside = jnp.logical_and(side == 0, first_cell[0] == 0)
    before = jnp.where(outside, received, take(hidden_a, side)[0])[None]
    rows, cell = tied(rows, cell)
    _, states[0, 0] = frame_step(
        before, w_sets[0], lows[0], size_a, tile, (cell,), edge=True
    )
    rows, held, states[0, 0] = tree_step(rows, held, orders[4], states[0, 0])
    rows, cell = tied(rows, cell)
    edge_b, cell = tied(edge_b, cell)
    _, states[0, 1] = frame_step(
        before, w_sets[1], lows[1], size_a, tile, (cell,), edge=True
    )

    across = head_swap(rows, 2)
    across, states = lax.optimization_barrier((across, states))
    shared = (rows, across, head_swap(rows, 1), head_swap(across, 1))
    anchor_b = project_kv(shared, (rows_a.shape[0], rows_b.shape[0]), w_b, size_b)
    att_b = attend_small(qkv_b, (first_cell, edge_b), anchor_b, size_b, ())
    crossing_b = head_swap(att_b, 2)
    states, att_b = lax.optimization_barrier((states, att_b))

    anchors = [project_kv(shared, (0, rows_a.shape[0]), w, size_a) for w in w_sets]
    queries = {0: lows, 1: tops}
    frames_x = {0: low, 1: high}
    pieces, theirs, mine = {}, {}, {}
    other_cell = jnp.bitwise_xor(rank_cell, 2)

    def attend_set(k, i):
        return attend_anchor(queries[k][i], anchors[i], states[k, i], size_a, tile)

    def send_columns(k):
        own, other, beside, diagonal = pieces[k]
        ordered = (other, own, diagonal, beside)
        return out_project(0, 1, other_cell, ordered, w_out_a, frames_x[k], None, ())

    own = [attend_set(1, 0), attend_set(1, 1)]
    pieces[1] = (*own, head_swap(own[0], 1), head_swap(own[1], 1))
    own = attend_set(0, 0)
    pieces[1], own = tied(pieces[1], own)
    sent = send_columns(1)
    states[0, 1], sent = tied(states[0, 1], sent)
    theirs[1] = head_swap(sent, 2)
    own = (own, attend_set(0, 1))
    pieces[0] = (*own, head_swap(own[0], 1), head_swap(own[1], 1))
    sent = send_columns(0)
    theirs[0] = head_swap(sent, 2)
    for k in (1, 0):
        pieces[k], sent = lax.optimization_barrier((pieces[k], sent))
        mine[k] = out_project(0, 1, rank_cell, pieces[k], w_out_a, frames_x[k], None, ())
    pieces_b = (att_b, crossing_b, head_swap(att_b, 1), head_swap(crossing_b, 1))
    out_b = out_project(0, frames, rank_cell, pieces_b, w_out_b, hidden_b, None, ())
    theirs[0], out_b = tied(theirs[0], out_b)
    near = jnp.concatenate([mine[0], mine[1]], axis=0)
    far_side = jnp.concatenate([theirs[0], theirs[1]], axis=0)
    out_a = jnp.where(
        side == 0,
        jnp.concatenate([near, far_side], axis=0),
        jnp.concatenate([far_side, near], axis=0),
    )
    return jnp.swapaxes(out_a, 1, 2), jnp.swapaxes(out_b, 1, 2)


def solution(mesh):
    in_specs = (
        P("frame", None, None),
        P(None, None, "head"),
        P(),
        P("frame", None, None),
        P(None, None, "head"),
        P(),
    )
    out_specs = (P("frame", None, "head"), P("frame", None, "head"))
    return jax.shard_map(shards, mesh=mesh, in_specs=in_specs, out_specs=out_specs, check_vma=False)
```

```python
import functools
import math

import jax
import jax.numpy as jnp
from jax import lax
from jax.experimental import pallas as pl
from jax.experimental.pallas import tpu as pltpu
from jax.sharding import PartitionSpec as P

HEADS = 8
F32 = jnp.float32
BF16 = jnp.bfloat16
NT = (((1,), (1,)), ((), ()))
ANY = pl.BlockSpec(memory_space=pl.ANY)
SMEM = pl.BlockSpec(memory_space=pltpu.SMEM)
SAFE_EXPONENT = 64.0
SAFE_VALUE = 2.0**30


def params(mib=24):
    return pltpu.CompilerParams(vmem_limit_bytes=mib * 2**20)


def cost(flops, bytes_accessed, exps=0):
    return pl.CostEstimate(
        flops=int(flops), bytes_accessed=int(bytes_accessed), transcendentals=int(exps)
    )


def whole(array):
    return pl.BlockSpec(array.shape, lambda *_: (0,) * len(array.shape))


def stored(shape):
    return pltpu.HBM(shape.shape, shape.dtype)


def far(array):
    return pltpu.with_memory_space_constraint(array, pltpu.HBM)


def normalize(rows):
    as_float = rows.astype(F32)
    centre = jnp.mean(as_float, axis=-1, keepdims=True)
    moved = as_float - centre
    spread = jnp.mean(jnp.square(moved), axis=-1, keepdims=True)
    return (moved * lax.rsqrt(spread + 1e-05)).astype(BF16)


def times(weights, normed):
    return lax.dot_general(weights, normed, NT, preferred_element_type=F32).astype(BF16)


def head_rows(local, size):
    row = lax.broadcasted_iota(jnp.int32, (8, local), 0)
    col = lax.broadcasted_iota(jnp.int32, (8, local), 1)
    return ((col >= row * size) & (col < (row + 1) * size)).astype(BF16)


def squares(array):
    as_float = array.astype(F32)
    return (as_float * as_float).astype(BF16)


def column_peaks(array, size):
    sums = jnp.dot(head_rows(array.shape[0], size), squares(array), preferred_element_type=F32)
    return jnp.broadcast_to(jnp.max(sums, axis=1, keepdims=True), (8, 128))


def row_peaks(array, size):
    sums = lax.dot_general(
        head_rows(array.shape[1], size), squares(array), NT, preferred_element_type=F32
    )
    return jnp.broadcast_to(jnp.max(sums, axis=1, keepdims=True), (8, 128))


def unless_extreme(peaks, values):
    largest = jnp.max(jnp.abs(values.astype(F32)))
    usual = (largest <= SAFE_VALUE) & (largest >= 1.0 / SAFE_VALUE)
    return jnp.where(usual, peaks, jnp.full_like(peaks, jnp.inf))


def within(q_peaks, k_peaks, scale):
    return jnp.max(q_peaks * k_peaks) * (1.05 * scale * scale) <= SAFE_EXPONENT**2


def project_body(x_ref, w_ref, *rest, size):
    q_ref, k_ref, v_ref, qn_ref, kn_ref, last_ref = rest[-6:]
    local = w_ref.shape[1]
    normed = normalize(x_ref[0])
    queries = times(w_ref[0], normed)
    q_ref[0] = queries
    qn_ref[0] = column_peaks(queries, size)
    keys = times(normed, w_ref[1])
    k_ref[0] = keys
    values = times(w_ref[2], normed)
    v_ref[0] = values
    kn_ref[0] = unless_extreme(row_peaks(keys, size), values)

    @pl.when(pl.program_id(0) == pl.num_programs(0) - 1)
    def _():
        last_ref[:local] = times(w_ref[1], normed)
        last_ref[local:] = values


def project(hidden, w, size, after):
    frames, seq, width = hidden.shape
    local = w.shape[1]
    col = jax.ShapeDtypeStruct((frames, local, seq), BF16)
    row = jax.ShapeDtypeStruct((frames, seq, local), BF16)
    last = jax.ShapeDtypeStruct((2 * local, seq), BF16)
    peak = jax.ShapeDtypeStruct((frames, 8, 128), F32)
    at = lambda f: (f, 0, 0)
    return pl.pallas_call(
        functools.partial(project_body, size=size),
        grid=(frames,),
        in_specs=[pl.BlockSpec((1, seq, width), at), whole(w)] + [SMEM] * len(after),
        out_specs=[
            pl.BlockSpec((1, local, seq), at),
            pl.BlockSpec((1, seq, local), at),
            pl.BlockSpec((1, local, seq), at),
            pl.BlockSpec((1, 8, 128), at),
            pl.BlockSpec((1, 8, 128), at),
            whole(last),
        ],
        out_shape=[stored(shape) for shape in (col, row, col, peak, peak, last)],
        compiler_params=params(),
        cost_estimate=cost(2 * 4 * frames * seq * width * local, frames * seq * width * 4),
    )(far(hidden), far(w), *after)


def project_kv_body(w_ref, *rest, size, rows):
    *x_refs, k_ref, v_ref, kn_ref = rest
    width = w_ref.shape[2]
    pieces = []
    for x_ref in x_refs:
        start, count, across = rows[0], rows[1], width // x_ref.shape[1]
        columns = [x_ref[start + i * count : start + (i + 1) * count] for i in range(across)]
        pieces.append(jnp.concatenate(columns, axis=1) if across > 1 else columns[0])
    normed = normalize(jnp.concatenate(pieces, axis=0))
    keys = times(normed, w_ref[1])
    k_ref[...] = keys
    values = times(w_ref[2], normed)
    v_ref[...] = values
    kn_ref[...] = unless_extreme(row_peaks(keys, size), values)


def project_kv(pieces, rows, w, size):
    seq = len(pieces) * rows[1]
    local, width = w.shape[1:]
    return pl.pallas_call(
        functools.partial(project_kv_body, size=size, rows=rows),
        out_shape=[
            jax.ShapeDtypeStruct((seq, local), BF16),
            jax.ShapeDtypeStruct((local, seq), BF16),
            jax.ShapeDtypeStruct((8, 128), F32),
        ],
        compiler_params=params(),
        cost_estimate=cost(2 * 3 * seq * width * local, seq * width * 4),
    )(w, *pieces)


def masked_queries(q, size):
    row = lax.broadcasted_iota(jnp.int32, q.shape, 0)
    zero = jnp.zeros_like(q)
    heads = q.shape[0] // size
    return [jnp.where((row >= h * size) & (row < (h + 1) * size), q, zero) for h in range(heads)]


def with_ones(v):
    return jnp.concatenate([v, jnp.ones((16, v.shape[1]), BF16)], axis=0)


def run_chunks(chunks, scale, tops, sums):
    def score(chunk):
        _, keys, queries, _ = chunk
        s = jnp.dot(keys, queries, preferred_element_type=F32)
        return s, jnp.max(s, axis=0, keepdims=True)

    ahead = score(chunks[0])
    for i, (h, _, _, values) in enumerate(chunks):
        s, top = ahead
        if i + 1 < len(chunks):
            ahead = score(chunks[i + 1])
        new = top if tops[h] is None else jnp.maximum(tops[h], top)
        weights = jnp.exp2((s - new) * scale).astype(BF16)
        part = jnp.dot(values, weights, preferred_element_type=F32)
        if tops[h] is not None:
            part = part + sums[h] * jnp.exp2((tops[h] - new) * scale)
        tops[h], sums[h] = new, part
    return tops, sums


def run_unshifted(chunks, scale, sums):
    for h, keys, queries, values in chunks:
        s = jnp.dot(keys, queries, preferred_element_type=F32)
        weights = jnp.exp2(s * scale).astype(BF16)
        part = jnp.dot(values, weights, preferred_element_type=F32)
        sums[h] = part if sums[h] is None else sums[h] + part
    return sums


def make_chunks(q, segments, size):
    queries = masked_queries(q, size)
    return [
        (h, keys, queries[h], with_ones(values[h * size : (h + 1) * size]))
        for h in range(len(queries))
        for keys, values in segments
    ]


def finish(o_ref, sums, size):
    for h in range(len(sums)):
        o_ref[pl.ds(h * size, size), :] = (sums[h][:size] / sums[h][size : size + 1]).astype(BF16)


def project_frame(x_ref, w_ref, q_ref, k_ref, v_ref, qn_ref, kn_ref, size):
    normed = normalize(x_ref[0])
    if q_ref is not None:
        queries = times(w_ref[0], normed)
        q_ref[...] = queries
        qn_ref[...] = column_peaks(queries, size)
    keys = times(normed, w_ref[1])
    k_ref[...] = keys
    values = times(w_ref[2], normed)
    v_ref[...] = values
    kn_ref[...] = unless_extreme(row_peaks(keys, size), values)
    return normed


def first_body(x_ref, w_ref, *rest, size):
    project_frame(x_ref, w_ref, *rest[-5:], size)


def step_body(x_ref, w_ref, qt_ref, k1, v1, qn1, kn1, *rest, size, scale, edge):
    if edge:
        k_ref, v_ref, kn_ref, st_ref = rest[-4:]
        results = (None, k_ref, v_ref, None, kn_ref)
    else:
        _, k_ref, v_ref, _, kn_ref, st_ref = rest[-6:]
        results = rest[-6:-1]

    @pl.when(pl.program_id(0) == 0)
    def _():
        project_frame(x_ref, w_ref, *results, size)

    segments = ((k1[...], v1[...]), (k_ref[...], v_ref[...]))
    peaks = jnp.maximum(kn1[...], kn_ref[...])
    attend_to_state(qt_ref[...], segments, qn1[...], peaks, st_ref, size, scale)


def frame_shapes(seq, local):
    return [
        jax.ShapeDtypeStruct((local, seq), BF16),
        jax.ShapeDtypeStruct((seq, local), BF16),
        jax.ShapeDtypeStruct((local, seq), BF16),
        jax.ShapeDtypeStruct((8, 128), F32),
        jax.ShapeDtypeStruct((8, 128), F32),
    ]


def project_first(rows, w, size, after):
    _, seq, width = rows.shape
    local = w.shape[1]
    shapes = frame_shapes(seq, local)
    return pl.pallas_call(
        functools.partial(first_body, size=size),
        grid=(1,),
        in_specs=[pl.BlockSpec((1, seq, width), lambda j: (0, 0, 0)), whole(w)]
        + [SMEM] * len(after),
        out_specs=[whole(shape) for shape in shapes],
        out_shape=[stored(shape) for shape in shapes],
        compiler_params=params(),
        cost_estimate=cost(2 * 3 * seq * width * local, seq * width * 4),
    )(far(rows), far(w), *after)


def frame_step(hidden, w, later, size, tile, after, edge=False):
    _, seq, width = hidden.shape
    local = w.shape[1]
    heads = local // size
    shapes = frame_shapes(seq, local)
    if edge:
        shapes = [shapes[1], shapes[2], shapes[4]]
    state = jax.ShapeDtypeStruct((heads, size + 16, seq), F32)
    *qkv, state = pl.pallas_call(
        functools.partial(
            step_body, size=size, scale=math.log2(math.e) / math.sqrt(size), edge=edge
        ),
        grid=(seq // tile,),
        in_specs=[
            pl.BlockSpec((1, seq, width), lambda j: (0, 0, 0)),
            whole(w),
            pl.BlockSpec((local, tile), lambda j: (0, j)),
            *[whole(part) for part in later[1:]],
        ]
        + [SMEM] * len(after),
        out_specs=[whole(shape) for shape in shapes]
        + [pl.BlockSpec((heads, size + 16, tile), lambda j: (0, 0, j))],
        out_shape=[stored(shape) for shape in shapes + [state]],
        compiler_params=params(),
        cost_estimate=cost(
            2 * 2 * heads * seq * 2 * seq * 256, 8 * seq * width, heads * 2 * seq * seq
        ),
    )(far(hidden), far(w), *map(far, later), *after)
    return qkv, state


def attend_to_state(q, segments, q_peaks, k_peaks, st_ref, size, scale):
    heads = q.shape[0] // size
    fits = within(q_peaks, k_peaks, scale)

    def keep(tops, sums):
        for h in range(heads):
            st_ref[h, : size + 8, :] = sums[h][: size + 8]
            st_ref[h, size + 8 :, :] = jnp.broadcast_to(tops[h], (8, q.shape[1]))

    @pl.when(fits)
    def _():
        sums = run_unshifted(make_chunks(q, segments, size), scale, [None] * heads)
        keep([jnp.zeros((1, q.shape[1]), F32)] * heads, sums)

    @pl.when(jnp.logical_not(fits))
    def _():
        chunks = make_chunks(q, segments, size)
        keep(*run_chunks(chunks, scale, [None] * heads, [None] * heads))


def anchor_body(q_ref, qn_ref, k_ref, v_ref, kn_ref, st_ref, *rest, size, scale):
    o_ref = rest[-1]
    heads = q_ref.shape[0] // size
    tops = [st_ref[h, size + 8 :, :] for h in range(heads)]
    unshifted = functools.reduce(jnp.maximum, [jnp.max(jnp.abs(t)) for t in tops]) == 0.0
    fits = jnp.logical_and(within(qn_ref[...], kn_ref[...], scale), unshifted)

    def start():
        chunks = make_chunks(q_ref[...], ((k_ref[...], v_ref[...]),), size)
        sums = [st_ref[h, : size + 8, :] for h in range(heads)]
        return chunks, [jnp.concatenate([s, s[size:]], axis=0) for s in sums]

    @pl.when(fits)
    def _():
        chunks, sums = start()
        finish(o_ref, run_unshifted(chunks, scale, sums), size)

    @pl.when(jnp.logical_not(fits))
    def _():
        chunks, sums = start()
        finish(o_ref, run_chunks(chunks, scale, [t[:1] for t in tops], sums)[1], size)


def attend_anchor(qkv, anchor, state, size, tile):
    q, _, _, qn, _ = qkv
    local, seq = q.shape
    heads = local // size
    return pl.pallas_call(
        functools.partial(anchor_body, size=size, scale=math.log2(math.e) / math.sqrt(size)),
        grid=(seq // tile,),
        in_specs=[
            pl.BlockSpec((local, tile), lambda j: (0, j)),
            whole(qn),
            *[whole(part) for part in anchor],
            pl.BlockSpec((heads, size + 16, tile), lambda j: (0, 0, j)),
        ],
        out_specs=pl.BlockSpec((local, tile), lambda j: (0, j)),
        out_shape=jax.ShapeDtypeStruct((local, seq), BF16),
        compiler_params=params(),
        cost_estimate=cost(
            2 * 2 * heads * seq * seq * 256, 8 * seq * local, heads * seq * seq
        ),
    )(q, qn, *anchor, state)


def small_body(first_ref, q_ref, ko, vo, kl, vl, edge, ka, va, *rest, size, scale):
    o_ref = rest[-1]
    start = pl.program_id(0) == 0
    outer = jnp.logical_and(start, first_ref[0] == 0)
    local = edge.shape[0] // 2
    kp = jnp.where(outer, edge[:local].T, kl[0])
    vp = jnp.where(outer, edge[local:], vl[0])
    heads = q_ref.shape[1] // size
    segments = ((ko[0], vo[0]), (kp, vp), (ka[...], va[...]))
    chunks = make_chunks(q_ref[0], segments, size)
    finish(o_ref, run_chunks(chunks, scale, [None] * heads, [None] * heads)[1], size)


def attend_small(qkv, edge, anchor, size, after):
    q, k, v, _, _ = qkv
    frames, local, seq = q.shape
    heads = local // size
    at = lambda f: (f, 0, 0)
    before = lambda f: (jnp.maximum(f - 1, 0), 0, 0)
    ks, vs = (1, seq, local), (1, local, seq)
    return pl.pallas_call(
        functools.partial(small_body, size=size, scale=math.log2(math.e) / math.sqrt(size)),
        grid=(frames,),
        in_specs=[
            SMEM,
            pl.BlockSpec((1, local, seq), at),
            pl.BlockSpec(ks, at),
            pl.BlockSpec(vs, at),
            pl.BlockSpec(ks, before),
            pl.BlockSpec(vs, before),
            whole(edge[1]),
            whole(anchor[0]),
            whole(anchor[1]),
        ]
        + [SMEM] * len(after),
        out_specs=pl.BlockSpec((local, seq), lambda f: (0, f)),
        out_shape=jax.ShapeDtypeStruct((local, frames * seq), BF16),
        compiler_params=params(),
        cost_estimate=cost(
            2 * 2 * frames * heads * seq * 3 * seq * 512,
            16 * frames * seq * local,
            frames * heads * seq * 3 * seq,
        ),
    )(edge[0], q, k, v, k, v, edge[1], *anchor[:2], *after)


def out_body(rank_ref, *rest):
    pieces, (w_ref, x_ref), o_ref = rest[:4], rest[4:6], rest[-3]
    w_own, attended = rest[-2:]
    rank = rank_ref[0]
    cols, width = w_own.shape
    pick = (
        lax.broadcasted_iota(jnp.int32, (cols, width), 1)
        == lax.broadcasted_iota(jnp.int32, (cols, width), 0) + rank * cols
    ).astype(BF16)

    @pl.when(pl.program_id(0) == 0)
    def _():
        w_own[...] = times(pick, w_ref[...])

    for bit, piece in zip((0, 2, 1, 3), pieces):
        start = pl.multiple_of(jnp.bitwise_xor(rank, bit) * cols, cols)
        attended[pl.ds(start, cols), :] = piece[...]
    total = jnp.dot(w_own[...], attended[...], preferred_element_type=F32)
    kept = lax.dot_general(pick, x_ref[0], NT, preferred_element_type=F32)
    o_ref[0] = (total + kept).astype(BF16)


def out_project(first, frames, rank, pieces, w, hidden, into, after):
    total_frames, seq, width = hidden.shape
    cols = pieces[0].shape[0]
    operands = [rank, *pieces, w, hidden]
    specs = [SMEM] + [pl.BlockSpec((cols, seq), lambda f: (0, f)) for _ in pieces]
    specs += [whole(w), pl.BlockSpec((1, seq, width), lambda f: (first + f, 0, 0))]
    aliases = {}
    if into is not None:
        aliases = {len(operands): 0}
        operands.append(into)
        specs.append(ANY)
    return pl.pallas_call(
        out_body,
        grid=(frames,),
        in_specs=specs + [SMEM] * len(after),
        out_specs=pl.BlockSpec((1, cols, seq), lambda f: (first + f, 0, 0)),
        out_shape=jax.ShapeDtypeStruct((total_frames, cols, seq), BF16),
        scratch_shapes=[pltpu.VMEM((cols, width), BF16), pltpu.VMEM((width, seq), BF16)],
        input_output_aliases=aliases,
        compiler_params=params(),
        cost_estimate=cost(2 * 2 * frames * seq * width * cols, 4 * frames * seq * width),
    )(*operands, *after)


def choose_body(receives_ref, got_ref, piece_ref, o_ref):
    o_ref[...] = jnp.where(receives_ref[0] == 1, got_ref[...], piece_ref[...])


def choose(receives, got, piece):
    return pl.pallas_call(
        choose_body,
        grid=(1,),
        in_specs=[SMEM, whole(got), whole(piece)],
        out_specs=whole(piece),
        out_shape=jax.ShapeDtypeStruct(piece.shape, piece.dtype),
        compiler_params=params(),
        cost_estimate=cost(0, 3 * 2 * piece.size),
    )(receives, got, piece)


def tree_step(piece, held, bits, done):
    heads = lax.axis_size("head")
    index, core = lax.axis_index("frame"), lax.axis_index("head") % 2
    pairs, masks, after = [], [], []
    for mine, bit in zip(held, bits):
        after.append(mine + [i ^ bit for i in mine])
        masks.append(sum(1 << (i ^ bit) for i in mine))
    for head in range(heads):
        bit = bits[head % 2]
        to = head ^ 2 if bit == 16 else head
        pairs += [(i * heads + head, (i ^ bit) * heads + to) for i in held[head % 2]]
    got = lax.ppermute(piece, ("frame", "head"), pairs)
    got, done = lax.optimization_barrier((got, done))
    mask = jnp.where(core == 0, jnp.uint32(masks[0]), jnp.uint32(masks[1]))
    receives = ((mask >> index.astype(jnp.uint32)) & 1).astype(jnp.int32).reshape(1)
    return choose(receives, got, piece), after, done


def head_swap(value, bit):
    peers = lax.axis_size("head")
    return lax.ppermute(value, "head", [(i, i ^ bit) for i in range(peers)])


def to_next(value):
    peers = lax.axis_size("frame")
    return lax.ppermute(value, "frame", [(i, i + 1) for i in range(peers - 1)])


def to_next_low(value):
    heads, peers = lax.axis_size("head"), lax.axis_size("frame")
    pairs = [
        (i * heads + h, (i + 1) * heads + h) for i in range(peers - 1) for h in range(heads // 2)
    ]
    return lax.ppermute(value, ("frame", "head"), pairs)


def take(hidden, frame):
    return lax.dynamic_slice(hidden, (frame, 0, 0), (1, *hidden.shape[1:]))


def edge_rows(hidden, rank):
    frames, seq, width = hidden.shape
    start = (frames - 1, (rank % 2) * (seq // 2), 0)
    return lax.dynamic_slice(hidden, start, (1, seq // 2, width))[0]


def quarter(hidden, rank):
    rows = hidden.shape[1] // lax.axis_size("head")
    return lax.dynamic_slice(hidden, (0, rank * rows, 0), (1, rows, hidden.shape[2]))[0]


def shards(hidden_a, w_qkv_a, w_out_a, hidden_b, w_qkv_b, w_out_b):
    rank = lax.axis_index("head")
    rank_cell = rank.astype(jnp.int32).reshape(1)
    first_cell = (lax.axis_index("frame") == 0).astype(jnp.int32).reshape(1)
    w_a, w_b = jnp.swapaxes(w_qkv_a, 1, 2), jnp.swapaxes(w_qkv_b, 1, 2)
    frames = hidden_a.shape[0]
    size_a, size_b = w_a.shape[1] // 2, w_b.shape[1] // 2
    tile = 512

    rows_a, rows_b = quarter(hidden_a, rank), quarter(hidden_b, rank)
    width = rows_a.shape[1]
    columns = [rows_b[:, i : i + width] for i in range(0, rows_b.shape[1], width)]
    rows = jnp.concatenate([rows_a, *columns], axis=0)
    held = [[0], [0]]
    orders = list(zip((8, 4, 16, 2, 1), (2, 1, 8, 4, 16)))

    cell = first_cell
    side = rank // 2
    w_sets = (w_a, head_swap(w_a, 2))
    low, high = (take(hidden_a, 2 * side + k) for k in range(2))

    def tied(value, cell):
        return lax.optimization_barrier((value, cell))

    tops, states = [None, None], {}
    tops[0] = list(project_first(high, w_sets[0], size_a, (cell,)))
    rows, held, tops[0][3] = tree_step(rows, held, orders[0], tops[0][3])
    rest, tops[0][3] = tied(edge_rows(hidden_a, rank), tops[0][3])
    edge_a = to_next_low(rest)

    rows, cell = tied(rows, cell)
    lows = [None, None]
    lows[0], states[1, 0] = frame_step(low, w_sets[0], tops[0], size_a, tile, (cell,))
    rows, held, states[1, 0] = tree_step(rows, held, orders[1], states[1, 0])

    rows, cell = tied(rows, cell)
    *qkv_b, last_b = project(hidden_b, w_b, size_b, (cell,))
    rows, held, last_b = tree_step(rows, held, orders[2], last_b)
    edge_b = to_next(last_b)

    rows, cell = tied(rows, cell)
    edge_a, cell = tied(edge_a, cell)
    tops[1] = project_first(high, w_sets[1], size_a, (cell,))
    lows[1], states[1, 1] = frame_step(low, w_sets[1], tops[1], size_a, tile, (cell,))
    rows, held, states[1, 1] = tree_step(rows, held, orders[3], states[1, 1])

    edge_a, states[1, 1] = tied(edge_a, states[1, 1])
    received = jnp.concatenate([edge_a, head_swap(edge_a, 1)], axis=0)
    outside = jnp.logical_and(side == 0, first_cell[0] == 0)
    before = jnp.where(outside, received, take(hidden_a, side)[0])[None]
    rows, cell = tied(rows, cell)
    _, states[0, 0] = frame_step(
        before, w_sets[0], lows[0], size_a, tile, (cell,), edge=True
    )
    rows, held, states[0, 0] = tree_step(rows, held, orders[4], states[0, 0])
    rows, cell = tied(rows, cell)
    edge_b, cell = tied(edge_b, cell)
    _, states[0, 1] = frame_step(
        before, w_sets[1], lows[1], size_a, tile, (cell,), edge=True
    )

    across = head_swap(rows, 2)
    across, states = lax.optimization_barrier((across, states))
    shared = (rows, across, head_swap(rows, 1), head_swap(across, 1))
    anchor_b = project_kv(shared, (rows_a.shape[0], rows_b.shape[0]), w_b, size_b)
    att_b = attend_small(qkv_b, (first_cell, edge_b), anchor_b, size_b, ())
    crossing_b = head_swap(att_b, 2)
    states, att_b = lax.optimization_barrier((states, att_b))

    anchors = [project_kv(shared, (0, rows_a.shape[0]), w, size_a) for w in w_sets]
    queries = {0: lows, 1: tops}
    frames_x = {0: low, 1: high}
    pieces, theirs, mine = {}, {}, {}
    other_cell = jnp.bitwise_xor(rank_cell, 2)

    def attend_set(k, i):
        return attend_anchor(queries[k][i], anchors[i], states[k, i], size_a, tile)

    def send_columns(k):
        own, other, beside, diagonal = pieces[k]
        ordered = (other, own, diagonal, beside)
        return out_project(0, 1, other_cell, ordered, w_out_a, frames_x[k], None, ())

    own = [attend_set(1, 0), attend_set(1, 1)]
    pieces[1] = (*own, head_swap(own[0], 1), head_swap(own[1], 1))
    own = attend_set(0, 0)
    pieces[1], own = tied(pieces[1], own)
    sent = send_columns(1)
    states[0, 1], sent = tied(states[0, 1], sent)
    theirs[1] = head_swap(sent, 2)
    own = (own, attend_set(0, 1))
    pieces[0] = (*own, head_swap(own[0], 1), head_swap(own[1], 1))
    sent = send_columns(0)
    theirs[0] = head_swap(sent, 2)
    pieces[1], theirs[1] = tied(pieces[1], theirs[1])
    for k in (1, 0):
        pieces[k], sent = lax.optimization_barrier((pieces[k], sent))
        mine[k] = out_project(0, 1, rank_cell, pieces[k], w_out_a, frames_x[k], None, ())
    pieces_b = (att_b, crossing_b, head_swap(att_b, 1), head_swap(crossing_b, 1))
    out_b = out_project(0, frames, rank_cell, pieces_b, w_out_b, hidden_b, None, ())
    theirs[0], out_b = tied(theirs[0], out_b)
    near = jnp.concatenate([mine[0], mine[1]], axis=0)
    far_side = jnp.concatenate([theirs[0], theirs[1]], axis=0)
    out_a = jnp.where(
        side == 0,
        jnp.concatenate([near, far_side], axis=0),
        jnp.concatenate([far_side, near], axis=0),
    )
    return jnp.swapaxes(out_a, 1, 2), jnp.swapaxes(out_b, 1, 2)


def solution(mesh):
    in_specs = (
        P("frame", None, None),
        P(None, None, "head"),
        P(),
        P("frame", None, None),
        P(None, None, "head"),
        P(),
    )
    out_specs = (P("frame", None, "head"), P("frame", None, "head"))
    return jax.shard_map(shards, mesh=mesh, in_specs=in_specs, out_specs=out_specs, check_vma=False)
```
